512 devices in a mesh: img: 32 (over y_hi, x, core), cap: 16 (over y_lo, z).
Axes of the slice: x: 4, y: 8 (y_hi: 4, y_lo: 2; y = y_hi * 2 + y_lo), z: 8, core: 2. Of those that a mesh axis runs over, the one named last changes fastest.
Arguments:
- image_student: bfloat16 [10240, 1024], P(('img', 'cap')), may hold values from -64 to 64
- caption_student: bfloat16 [10240, 1024], P(('cap', 'img')), may hold values from -64 to 64
- image_teacher: bfloat16 [10240, 768], P(('img', 'cap')), may hold values from -64 to 64
- caption_teacher: bfloat16 [10240, 768], P(('cap', 'img')), may hold values from -64 to 64
Outputs:
- image_grad: float32 [10240, 1024], P(('img', 'cap'))
- caption_grad: float32 [10240, 1024], P(('cap', 'img'))
The draws below stay inside these ranges and needn't reach their ends.
All inputs are finite; a program needn't handle non-finite values.
Results may differ from the reference program's by a relative error of at most 0.004.
Values may be sent and summed in bfloat16 or wider, within the bound.
A program may use at most 64 MiB of HBM per device.

```python
import math
import jax
import jax.numpy as jnp
from jax import lax

DS = 1024
DT = 768
ROWS = 320
BATCH = 10240


def aligned_pair(key, salt, width):
    key = jax.random.fold_in(key, salt)
    keys = jax.random.split(key, 5)
    images = jax.random.normal(keys[0], (BATCH, width), jnp.float32)
    captions = jax.random.normal(keys[1], (BATCH, width), jnp.float32)
    groups = 8
    stride = BATCH // 16
    first_col = jnp.arange(groups, dtype=jnp.int32) * stride + jax.random.randint(keys[4], (groups,), 0, stride)
    second_col = first_col + BATCH // 2
    first_row = first_col + BATCH // 4
    second_row = (first_col + 3 * (BATCH // 4)) % BATCH
    captions = captions.at[first_col].set(captions[first_col])
    captions = captions.at[second_col].set(captions[second_col])
    images = images.at[first_row].set(images[first_row])
    images = images.at[second_row].set(images[second_row])
    return (jnp.clip(images, -64.0, 64.0), jnp.clip(captions, -64.0, 64.0))


def draw_image_student(key, part):
    pair = aligned_pair(key, 101, DS)
    return pair[0].astype(jnp.bfloat16)


def draw_caption_student(key, part):
    pair = aligned_pair(key, 101, DS)
    return pair[1].astype(jnp.bfloat16)


def draw_image_teacher(key, part):
    pair = aligned_pair(key, 202, DT)
    return pair[0].astype(jnp.bfloat16)


def draw_caption_teacher(key, part):
    pair = aligned_pair(key, 202, DT)
    return pair[1].astype(jnp.bfloat16)


def setup_inputs(seed: int = 0) -> dict:
    splits = jax.random.split(jax.random.key(seed), 5)
    image_student = draw_image_student(jax.random.fold_in(splits[4], 71), 0)
    caption_student = draw_caption_student(jax.random.fold_in(splits[4], 71), 0)
    image_teacher = draw_image_teacher(jax.random.fold_in(splits[4], 71), 0)
    caption_teacher = draw_caption_teacher(jax.random.fold_in(splits[4], 71), 0)
    return dict(image_student=image_student, caption_student=caption_student, image_teacher=image_teacher, caption_teacher=caption_teacher)


def logits(left, right, factor):
    return factor * jnp.dot(left, right.T, preferred_element_type=jnp.float32)

def reference(image_student, caption_student, image_teacher, caption_teacher):
    student_gain = 3.0 / math.sqrt(DS)
    teacher_gain = 3.0 / math.sqrt(DT)
    blocks = BATCH // ROWS
    block_student = image_student.reshape(blocks, ROWS, DS)
    block_teacher = image_teacher.reshape(blocks, ROWS, DT)
    block_index = jnp.arange(blocks, dtype=jnp.int32)

    def first_pass(running, inputs):
        peak_s, total_s, peak_t, total_t = running
        rows_student, rows_teacher = inputs
        student = logits(rows_student, caption_student, student_gain)
        teacher = logits(rows_teacher, caption_teacher, teacher_gain)
        results = []
        for matrix in (student, teacher):
            row_peak = lax.optimization_barrier(jnp.max(matrix, axis=1))
            results.append(row_peak + jnp.log(lax.optimization_barrier(jnp.sum(jnp.exp(matrix - row_peak[:, None]), axis=1))))
        new_state = []
        for matrix, old_peak, old_total in ((student, peak_s, total_s), (teacher, peak_t, total_t)):
            col_peak = lax.optimization_barrier(jnp.max(matrix, axis=0))
            col_total = lax.optimization_barrier(jnp.sum(jnp.exp(matrix - col_peak[None, :]), axis=0))
            merged = jnp.maximum(old_peak, col_peak)
            new_state.append(merged)
            new_state.append(old_total * jnp.exp(old_peak - merged) + col_total * jnp.exp(col_peak - merged))
        return (tuple(new_state), (results[0], results[1]))
    start_peak = jnp.full((BATCH,), -jnp.inf, jnp.float32)
    start_total = jnp.zeros((BATCH,), jnp.float32)
    state, row_lses = lax.scan(first_pass, (start_peak, start_total, start_peak, start_total), (block_student, block_teacher))
    col_lse_student = state[0] + jnp.log(state[1])
    col_lse_teacher = state[2] + jnp.log(state[3])
    column_ids = jnp.arange(BATCH, dtype=jnp.int32)

    def second_pass(caption_acc, inputs):
        rows_student, rows_teacher, lse_student, lse_teacher, which = inputs
        student = logits(rows_student, caption_student, student_gain)
        teacher = logits(rows_teacher, caption_teacher, teacher_gain)
        row_ids = which * ROWS + jnp.arange(ROWS, dtype=jnp.int32)
        diag_mask = (row_ids[:, None] == column_ids[None, :]).astype(jnp.float32)
        tile_grad = 0.5 * (jnp.exp(student - lse_student[:, None]) + jnp.exp(student - col_lse_student[None, :]))
        tile_grad = tile_grad - 0.25 * (jnp.exp(teacher - lse_teacher[:, None]) + jnp.exp(teacher - col_lse_teacher[None, :]))
        tile_grad = (tile_grad - 0.5 * diag_mask).astype(jnp.bfloat16)
        image_part = jnp.dot(tile_grad, caption_student, preferred_element_type=jnp.float32)
        caption_acc = caption_acc + jnp.dot(tile_grad.T, rows_student, preferred_element_type=jnp.float32)
        return (caption_acc, image_part)
    caption_grad, image_parts = lax.scan(second_pass, jnp.zeros((BATCH, DS), jnp.float32), (block_student, block_teacher, row_lses[0], row_lses[1], block_index))
    return (image_parts.reshape(BATCH, DS), caption_grad)
```

```python
import math

import jax
import jax.numpy as jnp
from jax import lax
from jax.experimental import pallas as pl
from jax.experimental.pallas import tpu as pltpu
from jax.sharding import PartitionSpec as P

MESH = pl.DeviceIdType.MESH
GAIN = 3.0
NX, NYH, NZ = 4, 4, 8
NI, NC = 2 * NZ, 2 * NX * NYH
DS, DT = 1024, 768
W = DS + DT + 512
WG = DS + 256
B = 20
RI, RC = 16 * NI, 16 * NC
MI, MC = 20 * NI, 20 * NC
LI = 384
BF, F32 = jnp.bfloat16, jnp.float32


def dot_t(a, b):
    return lax.dot_general(a, b, (((1,), (1,)), ((), ())), preferred_element_type=F32)


def t_dot(a, b):
    return lax.dot_general(a, b, (((0,), (0,)), ((), ())), preferred_element_type=F32)


def fold_matrix():
    a = lax.broadcasted_iota(jnp.int32, (256, 256), 0)
    b = lax.broadcasted_iota(jnp.int32, (256, 256), 1)
    source = 16 * ((a >> 2) & 15) + 4 * (a >> 6) + (a & 3)
    return jnp.where(b == source, 1.0, 0.0).astype(BF)


def kernel(
    is_ref, cs_ref, it_ref, ct_ref, oi_ref, oc_ref,
    gi, gc, ar, br, rp, es, et, fs, ft, rmx, tb, tb2, rxr, rxc,
    tg, pi, si, ri, pc, sc, r_core, s_x, r_x, s_y, r_y,
    gi_r, gi_s, gc_r, gc_s, lr_r, lr_s, lc_r, lc_s,
    ri_r, ri_s, co_r, co_s, x_r, x_s, y_r, y_s,
):
    img, cap = lax.axis_index("img"), lax.axis_index("cap")
    yh, x, core = img // (2 * NX), (img // 2) % NX, img % 2
    yl, z = cap // NZ, cap % NZ

    def at_img(dyh, dx, dcore):
        return (((yh + dyh) % NYH) * NX + (x + dx) % NX) * 2 + (core + dcore) % 2

    def slot_c(dyh, dx, dcore):
        return ((core + dcore) % 2) * (NX * NYH) + ((x + dx) % NX) * NYH + (yh + dyh) % NYH

    def at_cap(dyl, dz):
        return ((yl + dyl) % 2) * NZ + (z + dz) % NZ

    def remote(src, dst, send, recv, dev):
        return pltpu.make_async_remote_copy(
            src_ref=src, dst_ref=dst, send_sem=send, recv_sem=recv, device_id=dev, device_id_type=MESH
        )

    up, down, pair = (img, at_cap(0, 1)), (img, at_cap(0, -1)), (img, at_cap(1, 0))
    xu, xd, x2 = (at_img(0, 1, 0), cap), (at_img(0, -1, 0), cap), (at_img(0, 2, 0), cap)
    sib = (at_img(0, 0, 1), cap)
    ys = [(at_img(d, 0, 0), cap) for d in (1, 2, 3)]

    barrier = pltpu.get_barrier_semaphore()
    near = [up, down, pair, xu, xd, x2, sib] + ys
    for dev in near:
        pl.semaphore_signal(barrier, inc=1, device_id=dev, device_id_type=MESH)

    me_i, me_c = cap, slot_c(0, 0, 0)
    for s_ref, t_ref, buf, slot in ((is_ref, it_ref, gi, me_i), (cs_ref, ct_ref, gc, me_c)):
        rows = pl.ds(pl.multiple_of(16 * slot, 16), 16)
        buf[rows, 0:DS] = s_ref[0:16, :]
        buf[rows, DS : DS + DT] = t_ref[0:16, :]
        s4 = s_ref[...].astype(F32)[16:20, :]
        t4 = t_ref[...].astype(F32)[16:20, :]
        rp[...] = jnp.zeros_like(rp)
        for q in range(4):
            rp[4 * q : 4 * q + 4, 0:256] = s4[:, 256 * q : 256 * q + 256]
        for q in range(3):
            rp[4 * q : 4 * q + 4, 256:512] = t4[:, 256 * q : 256 * q + 256]
        buf[rows, DS + DT : W] = rp[...].astype(BF)

    pl.semaphore_wait(barrier, len(near))

    pending = []

    def gi_at(slot):
        return gi.at[pl.ds(pl.multiple_of(16 * slot, 16), 16), :]

    def gc_at(slot):
        return gc.at[pl.ds(pl.multiple_of(16 * slot, 16), 16), :]

    count = {"i": 0, "c": 0}

    def send_i(slot, *devs):
        for dev in devs:
            c = remote(gi_at(slot), gi_at(slot), gi_s.at[count["i"]], gi_r.at[slot], dev)
            count["i"] += 1
            c.start()
            pending.append(c)

    def send_c(slot, *devs):
        for dev in devs:
            c = remote(gc_at(slot), gc_at(slot), gc_s.at[count["c"]], gc_r.at[slot], dev)
            count["c"] += 1
            c.start()
            pending.append(c)

    def got_i(slot):
        remote(gi_at(slot), gi_at(slot), gi_s.at[0], gi_r.at[slot], up).wait_recv()

    def got_c(slot):
        remote(gc_at(slot), gc_at(slot), gc_s.at[0], gc_r.at[slot], up).wait_recv()

    def img_own_up(k):
        s = at_cap(0, -k)
        got_i(s)
        if k < 4:
            send_i(s, up)

    def img_own_down(k):
        s = at_cap(0, k)
        got_i(s)
        if k < 3:
            send_i(s, down)

    def img_pair_up(k):
        s = at_cap(1, -k)
        got_i(s)
        if k < 3:
            send_i(s, up)

    def img_pair_down(k):
        s = at_cap(1, k)
        got_i(s)
        if k < 4:
            send_i(s, down)

    def cap_y(j):
        s = slot_c(j, 0, 0)
        got_c(s)
        send_c(s, xu, xd, sib)

    def cap_xu(j):
        s = slot_c(j, -1, 0)
        got_c(s)
        if j < 2:
            send_c(s, xu)
        send_c(s, sib)

    def cap_xd(j):
        s = slot_c(j, 1, 0)
        got_c(s)
        if j >= 2:
            send_c(s, xd)
        send_c(s, sib)

    def cap_x2(j):
        s = slot_c(j, 2, 0)
        got_c(s)
        send_c(s, sib)

    send_i(me_i, pair)
    send_c(me_c, *ys)
    send_i(me_i, up, down)
    send_c(me_c, xu, xd, sib)

    s = at_cap(1, 0)
    got_i(s)
    send_i(s, up, down)
    img_own_up(1)
    img_own_down(1)
    cap_xu(0)
    cap_xd(0)
    cap_y(1)
    cap_y(3)
    img_pair_up(1)
    img_pair_down(1)
    cap_y(2)
    img_own_up(2)
    img_own_down(2)
    cap_xu(1)
    cap_xd(3)
    cap_x2(0)
    img_pair_up(2)
    img_pair_down(2)
    cap_xu(3)
    cap_xd(1)
    img_own_up(3)
    img_own_down(3)
    cap_xu(2)
    cap_xd(2)
    img_pair_up(3)
    img_pair_down(3)
    cap_x2(3)
    cap_x2(1)
    cap_x2(2)
    img_own_up(4)
    img_pair_down(4)
    for dx in range(NX):
        for j in range(NYH):
            got_c(slot_c(j, dx, 1))

    fold = fold_matrix()
    for src, base, dst, off in ((gi, 0, ar, 0), (gc, 0, br, 0), (gc, 256, br, 64)):
        for g, n in ((0, 4), (1, 3)):
            cols = DS + DT + 256 * g
            y = jnp.dot(fold, src[base : base + 256, cols : cols + 256], preferred_element_type=F32).astype(BF)
            for q in range(n):
                c = 256 * (4 * g + q)
                dst[off : off + 64, c : c + 256] = y[64 * q : 64 * q + 64, :]

    row_lse, col_lse, col_max = [], [], []
    for k, (e_row, e_col, lo, width) in enumerate(((es, fs, 0, DS), (et, ft, DS, DT))):
        gain = GAIN / math.sqrt(width)
        cols = slice(lo, lo + width)
        e_col[0:RI, 0:RC] = gain * dot_t(gi[:, cols], gc[:, cols])
        e_col[0:RI, RC:MC] = gain * dot_t(gi[:, cols], br[:, cols])
        e_col[RI:MI, 0:RC] = gain * dot_t(ar[:, cols], gc[:, cols])
        e_col[RI:MI, RC:MC] = gain * dot_t(ar[:, cols], br[:, cols])
        top = None
        lses = []
        for b in range(0, MI, 64):
            blk = e_col[b : b + 64, :]
            m = jnp.max(blk, axis=1, keepdims=True)
            rmx[k, b : b + 64, :] = m
            e = jnp.exp(blk - m)
            e_row[b : b + 64, :] = e
            lses.append(m + jnp.log(jnp.sum(e, axis=1, keepdims=True)))
            t = jnp.max(blk, axis=0, keepdims=True)
            top = t if top is None else jnp.maximum(top, t)
        row_lse.append(lses)
        total = None
        for b in range(0, MI, 64):
            e = jnp.exp(e_col[b : b + 64, :] - top)
            e_col[b : b + 64, :] = e
            t = jnp.sum(e, axis=0, keepdims=True)
            total = t if total is None else total + t
        col_max.append(top)
        col_lse.append(top + jnp.log(total))

    lane = lax.broadcasted_iota(jnp.int32, (64, 128), 1)
    for n, b in enumerate(range(0, MI, 64)):
        tb[b : b + 64, :] = jnp.where(lane == 0, row_lse[0][n], jnp.where(lane == 1, row_lse[1][n], 0.0))
    tb[MI:LI, :] = jnp.zeros((LI - MI, 128), F32)
    rxr[me_i] = tb[...].T[0:2, :]
    rxc[me_c, 0:1, :] = col_lse[0]
    rxc[me_c, 1:2, :] = col_lse[1]

    for j in range(NYH):
        for dx in range(NX):
            for dc in range(2):
                if (j, dx, dc) != (0, 0, 0):
                    n = (j * NX + dx) * 2 + dc
                    c = remote(rxc.at[me_c], rxc.at[me_c], lc_s.at[n], lc_r.at[me_c], (at_img(j, dx, dc), cap))
                    c.start()
                    pending.append(c)
    for dy in range(2):
        for dz in range(NZ):
            if (dy, dz) != (0, 0):
                n = dy * NZ + dz
                c = remote(rxr.at[me_i], rxr.at[me_i], lr_s.at[n], lr_r.at[me_i], (img, at_cap(dy, dz)))
                c.start()
                pending.append(c)
    for dy in range(2):
        for dz in range(NZ):
            if (dy, dz) != (0, 0):
                s = at_cap(dy, dz)
                remote(rxr.at[s], rxr.at[s], lr_s.at[0], lr_r.at[s], up).wait_recv()
    for j in range(NYH):
        for dx in range(NX):
            for dc in range(2):
                if (j, dx, dc) != (0, 0, 0):
                    s = slot_c(j, dx, dc)
                    remote(rxc.at[s], rxc.at[s], lc_s.at[0], lc_r.at[s], up).wait_recv()

    def pool(parts):
        m = jnp.max(parts, axis=0)
        return m + jnp.log(jnp.sum(jnp.exp(parts - m[None]), axis=0))

    tb2[...] = jnp.zeros_like(tb2)
    tb2[0:2, :] = pool(rxr[...])
    rows_all = tb2[...].T
    cols_all = pool(rxc[...])
    f_col_s = 0.5 * jnp.exp(col_max[0] - cols_all[0:1, :])
    f_col_t = 0.25 * jnp.exp(col_max[1] - cols_all[1:2, :])

    b = lax.broadcasted_iota(jnp.int32, (1, MC), 1)
    t = jnp.where(b < RC, b >> 4, (b - RC) >> 2)
    u = jnp.where(b < RC, b & 15, 16 + (b & 3))
    block = (t & 3) * (2 * NX) + ((t >> 2) & 3) * 2 + (t >> 4)
    col_id = cap * MC + block * B + u
    for lo in range(0, MI, 64):
        a = lo + lax.broadcasted_iota(jnp.int32, (64, 1), 0)
        if lo < RI:
            row_id = img * MI + (a >> 4) * B + (a & 15)
        else:
            row_id = img * MI + ((a - RI) >> 2) * B + 16 + (a & 3)
        rows = slice(lo, lo + 64)
        f_row_s = 0.5 * jnp.exp(rmx[0, rows, :] - rows_all[rows, 0:1])
        f_row_t = 0.25 * jnp.exp(rmx[1, rows, :] - rows_all[rows, 1:2])
        g = es[rows, :] * f_row_s + fs[rows, :] * f_col_s
        g = g - (et[rows, :] * f_row_t + ft[rows, :] * f_col_t)
        g = g - jnp.where(row_id == col_id, 0.5, 0.0)
        tg[rows, :] = g.astype(BF)

    pc[...] = t_dot(tg[0:RI, :], gi[:, 0:DS]) + t_dot(tg[RI:MI, :], ar[:, 0:DS])
    for h in range(2):
        rows = slice(256 * h, 256 * h + 256)
        sc[rows, 0:DS] = pc[rows, :]
        rem = jnp.concatenate(
            [pc[RC + 64 * h : RC + 64 * h + 64, 256 * q : 256 * q + 256] for q in range(4)], axis=0
        ).astype(BF)
        sc[rows, DS:WG] = t_dot(fold, rem)
    half = NX * NYH * 16
    core_copies = []
    for n, dx in enumerate((2, 1, 3, 0)):
        there = pl.ds(pl.multiple_of((1 - core) * half + ((x + dx) % NX) * (NYH * 16), 64), 64)
        c = remote(sc.at[there, :], r_core.at[n], co_s.at[n], co_r.at[n], sib)
        c.start()
        core_copies.append(c)
        pending.append(c)

    pi[...] = jnp.dot(tg[:, 0:RC], gc[:, 0:DS], preferred_element_type=F32) + jnp.dot(
        tg[:, RC:MC], br[:, 0:DS], preferred_element_type=F32
    )
    si[:, 0:DS] = pi[0:RI, :].astype(BF)
    rem = jnp.concatenate([pi[RI:MI, 256 * q : 256 * q + 256] for q in range(4)], axis=0).astype(BF)
    si[:, DS:WG] = t_dot(fold, rem).astype(BF)
    for dz in (4, 3, 5, 2, 6, 1, 7, 0):
        for dy in range(2):
            if (dy, dz) != (0, 0):
                n = dy * NZ + dz
                s = at_cap(dy, dz)
                block = si.at[pl.ds(pl.multiple_of(16 * s, 16), 16), :]
                c = remote(block, ri.at[me_i], ri_s.at[n], ri_r.at[me_i], (img, s))
                c.start()
                pending.append(c)

    for n, dx in enumerate((2, 1, 3, 0)):
        here = pl.ds(pl.multiple_of(core * half + ((x + dx) % NX) * (NYH * 16), 64), 64)
        core_copies[n].wait_recv()
        v = sc[here, :] + r_core[n]
        if dx:
            s_x[n] = v.astype(BF)
            dev = (x2, xu, xd)[n]
            c = remote(s_x.at[n], r_x.at[n], x_s.at[n], x_r.at[n], dev)
            c.start()
            pending.append(c)
        else:
            pc[0:64, :] = v[:, 0:DS]
            pc[64:128, 0:256] = v[:, DS:WG]
    for n in range(3):
        remote(r_x.at[n], r_x.at[n], x_s.at[n], x_r.at[n], up).wait_recv()
    main, rest = pc[0:64, :], pc[64:128, 0:256]
    for n in range(3):
        main = main + r_x[n, :, 0:DS].astype(F32)
        rest = rest + r_x[n, :, DS:WG].astype(F32)
    s_y[:, 0:DS] = main
    s_y[:, DS:WG] = rest
    for n, d in enumerate((2, 1, 3)):
        there = pl.ds(pl.multiple_of(16 * ((yh + d) % NYH), 16), 16)
        s_x[3, 16 * n : 16 * n + 16, :] = s_y[there, :].astype(BF)
        c = remote(s_x.at[3, pl.ds(16 * n, 16), :], r_y.at[n], y_s.at[n], y_r.at[n], ys[d - 1])
        c.start()
        pending.append(c)

    def unfold(acc, out):
        out[0:16, :] = acc[:, 0:DS]
        for q in range(4):
            out[16:20, 256 * q : 256 * q + 256] = acc[4 * q : 4 * q + 4, DS:WG]

    for dy in range(2):
        for dz in range(NZ):
            if (dy, dz) != (0, 0):
                s = at_cap(dy, dz)
                remote(ri.at[s], ri.at[s], ri_s.at[0], ri_r.at[s], up).wait_recv()
    ri[me_i] = si[pl.ds(pl.multiple_of(16 * me_i, 16), 16), :]
    acc = ri[0].astype(F32)
    for n in range(1, NI):
        acc = acc + ri[n].astype(F32)
    unfold(acc, oi_ref)

    acc = s_y[pl.ds(pl.multiple_of(16 * yh, 16), 16), :]
    for n in range(3):
        remote(r_y.at[n], r_y.at[n], y_s.at[n], y_r.at[n], up).wait_recv()
        acc = acc + r_y[n].astype(F32)
    unfold(acc, oc_ref)

    for c in pending:
        c.wait_send()


def local(image_student, caption_student, image_teacher, caption_teacher):
    vmem = pl.BlockSpec(memory_space=pltpu.VMEM)
    dma = pltpu.SemaphoreType.DMA
    out = jax.ShapeDtypeStruct((B, DS), F32)
    return pl.pallas_call(
        kernel,
        out_shape=(out, out),
        in_specs=[vmem] * 4,
        out_specs=(vmem, vmem),
        scratch_shapes=[
            pltpu.VMEM((RI, W), BF),
            pltpu.VMEM((RC, W), BF),
            pltpu.VMEM((MI - RI, DS + DT), BF),
            pltpu.VMEM((MC - RC, DS + DT), BF),
            pltpu.VMEM((16, 512), F32),
            pltpu.VMEM((MI, MC), F32),
            pltpu.VMEM((MI, MC), F32),
            pltpu.VMEM((MI, MC), F32),
            pltpu.VMEM((MI, MC), F32),
            pltpu.VMEM((2, MI, 1), F32),
            pltpu.VMEM((LI, 128), F32),
            pltpu.VMEM((128, LI), F32),
            pltpu.VMEM((NI, 2, LI), F32),
            pltpu.VMEM((NC, 2, MC), F32),
            pltpu.VMEM((MI, MC), BF),
            pltpu.VMEM((MI, DS), F32),
            pltpu.VMEM((RI, WG), BF),
            pltpu.VMEM((NI, 16, WG), BF),
            pltpu.VMEM((MC, DS), F32),
            pltpu.VMEM((RC, WG), F32),
            pltpu.VMEM((4, 64, WG), F32),
            pltpu.VMEM((4, 64, WG), BF),
            pltpu.VMEM((3, 64, WG), BF),
            pltpu.VMEM((64, WG), F32),
            pltpu.VMEM((3, 16, WG), BF),
            dma((NI,)), dma((15,)), dma((NC,)), dma((34,)),
            dma((NI,)), dma((NI,)), dma((NC,)), dma((NC,)),
            dma((NI,)), dma((NI,)), dma((4,)), dma((4,)),
            dma((3,)), dma((3,)), dma((3,)), dma((3,)),
        ],
        compiler_params=pltpu.CompilerParams(
            collective_id=0, has_side_effects=True, vmem_limit_bytes=48 * 2**20
        ),
        cost_estimate=pl.CostEstimate(flops=1_600_000_000, bytes_accessed=400_000, transcendentals=900_000),
        name="contrastive",
    )(image_student, caption_student, image_teacher, caption_teacher)


def solution(mesh):
    return jax.shard_map(
        local,
        mesh=mesh,
        in_specs=(
            P(("img", "cap"), None),
            P(("cap", "img"), None),
            P(("img", "cap"), None),
            P(("cap", "img"), None),
        ),
        out_specs=(P(("img", "cap"), None), P(("cap", "img"), None)),
        check_vma=False,
    )
```

```python
import math

import jax
import jax.numpy as jnp
from jax import lax
from jax.experimental import pallas as pl
from jax.experimental.pallas import tpu as pltpu
from jax.sharding import PartitionSpec as P

MESH = pl.DeviceIdType.MESH
GAIN = 3.0
NX, NYH, NZ = 4, 4, 8
NI, NC = 2 * NZ, 2 * NX * NYH
DS, DT = 1024, 768
W = DS + DT + 512
WG = DS + 256
B = 20
RI, RC = 16 * NI, 16 * NC
MI, MC = 20 * NI, 20 * NC
LI = 384
BF, F32 = jnp.bfloat16, jnp.float32


def dot_t(a, b):
    return lax.dot_general(a, b, (((1,), (1,)), ((), ())), preferred_element_type=F32)


def t_dot(a, b):
    return lax.dot_general(a, b, (((0,), (0,)), ((), ())), preferred_element_type=F32)


def fold_matrix():
    a = lax.broadcasted_iota(jnp.int32, (256, 256), 0)
    b = lax.broadcasted_iota(jnp.int32, (256, 256), 1)
    source = 16 * ((a >> 2) & 15) + 4 * (a >> 6) + (a & 3)
    return jnp.where(b == source, 1.0, 0.0).astype(BF)


def kernel(
    is_hbm, cs_hbm, it_hbm, ct_hbm, oi_ref, oc_ref,
    is_ref, cs_ref, it_ref, ct_ref,
    gi, gc, ar, br, rp, es, et, fs, ft, rmx, tb, tb2, rxr, rxc, rxr2, rxc2,
    tg, pi, si, s_p, r_p, s_z, r_z, pc, sc, r_core, s_x, r_x, s_y, r_y,
    in_sem, gi_r, gi_s, gc_r, gc_s, lr_r, lr_s, lc_r, lc_s, mr_r, mr_s, mc_r, mc_s,
    p_r, p_s, z_r, z_s, co_r, co_s, x_r, x_s, y_r, y_s,
):
    img, cap = lax.axis_index("img"), lax.axis_index("cap")
    yh, x, core = img // (2 * NX), (img // 2) % NX, img % 2
    yl, z = cap // NZ, cap % NZ

    def at_img(dyh, dx, dcore):
        return (((yh + dyh) % NYH) * NX + (x + dx) % NX) * 2 + (core + dcore) % 2

    def slot_c(dyh, dx, dcore):
        return ((core + dcore) % 2) * (NX * NYH) + ((x + dx) % NX) * NYH + (yh + dyh) % NYH

    def at_cap(dyl, dz):
        return ((yl + dyl) % 2) * NZ + (z + dz) % NZ

    def remote(src, dst, send, recv, dev):
        return pltpu.make_async_remote_copy(
            src_ref=src, dst_ref=dst, send_sem=send, recv_sem=recv, device_id=dev, device_id_type=MESH
        )

    up, down, pair = (img, at_cap(0, 1)), (img, at_cap(0, -1)), (img, at_cap(1, 0))
    xu, xd, x2 = (at_img(0, 1, 0), cap), (at_img(0, -1, 0), cap), (at_img(0, 2, 0), cap)
    sib = (at_img(0, 0, 1), cap)
    ys = [(at_img(d, 0, 0), cap) for d in (1, 2, 3)]

    barrier = pltpu.get_barrier_semaphore()
    near = [up, down, pair, xu, xd, x2, sib] + ys
    for dev in near:
        pl.semaphore_signal(barrier, inc=1, device_id=dev, device_id_type=MESH)

    loads = []
    for n, (src, dst) in enumerate(((is_hbm, is_ref), (cs_hbm, cs_ref), (it_hbm, it_ref), (ct_hbm, ct_ref))):
        c = pltpu.make_async_copy(src, dst, in_sem.at[n])
        c.start()
        loads.append(c)
    for c in loads:
        c.wait()

    me_i, me_c = cap, slot_c(0, 0, 0)
    for s_ref, t_ref, buf, slot in ((is_ref, it_ref, gi, me_i), (cs_ref, ct_ref, gc, me_c)):
        rows = pl.ds(pl.multiple_of(16 * slot, 16), 16)
        buf[rows, 0:DS] = s_ref[0:16, :]
        buf[rows, DS : DS + DT] = t_ref[0:16, :]
        s4 = s_ref[...].astype(F32)[16:20, :]
        t4 = t_ref[...].astype(F32)[16:20, :]
        rp[...] = jnp.zeros_like(rp)
        for q in range(4):
            rp[4 * q : 4 * q + 4, 0:256] = s4[:, 256 * q : 256 * q + 256]
        for q in range(3):
            rp[4 * q : 4 * q + 4, 256:512] = t4[:, 256 * q : 256 * q + 256]
        buf[rows, DS + DT : W] = rp[...].astype(BF)

    pl.semaphore_wait(barrier, len(near))

    pending = []

    def gi_at(slot):
        return gi.at[pl.ds(pl.multiple_of(16 * slot, 16), 16), :]

    def gc_at(slot):
        return gc.at[pl.ds(pl.multiple_of(16 * slot, 16), 16), :]

    count = {"i": 0, "c": 0}

    def send_i(slot, *devs):
        for dev in devs:
            c = remote(gi_at(slot), gi_at(slot), gi_s.at[count["i"]], gi_r.at[slot], dev)
            count["i"] += 1
            c.start()
            pending.append(c)

    def send_c(slot, *devs):
        for dev in devs:
            c = remote(gc_at(slot), gc_at(slot), gc_s.at[count["c"]], gc_r.at[slot], dev)
            count["c"] += 1
            c.start()
            pending.append(c)

    def got_i(slot):
        remote(gi_at(slot), gi_at(slot), gi_s.at[0], gi_r.at[slot], up).wait_recv()

    def got_c(slot):
        remote(gc_at(slot), gc_at(slot), gc_s.at[0], gc_r.at[slot], up).wait_recv()

    def img_own_up(k):
        s = at_cap(0, -k)
        got_i(s)
        if k < 4:
            send_i(s, up)

    def img_own_down(k):
        s = at_cap(0, k)
        got_i(s)
        if k < 3:
            send_i(s, down)

    def img_pair_up(k):
        s = at_cap(1, -k)
        got_i(s)
        if k < 3:
            send_i(s, up)

    def img_pair_down(k):
        s = at_cap(1, k)
        got_i(s)
        if k < 4:
            send_i(s, down)

    def cap_y(j):
        s = slot_c(j, 0, 0)
        got_c(s)
        send_c(s, xu, xd, sib)

    def cap_xu(j):
        s = slot_c(j, -1, 0)
        got_c(s)
        if j < 2:
            send_c(s, xu)
        send_c(s, sib)

    def cap_xd(j):
        s = slot_c(j, 1, 0)
        got_c(s)
        if j >= 2:
            send_c(s, xd)
        send_c(s, sib)

    def cap_x2(j):
        s = slot_c(j, 2, 0)
        got_c(s)
        send_c(s, sib)

    send_i(me_i, pair)
    send_c(me_c, *ys)
    send_i(me_i, up, down)
    send_c(me_c, xu, xd, sib)

    s = at_cap(1, 0)
    got_i(s)
    send_i(s, up, down)
    img_own_up(1)
    img_own_down(1)
    cap_xu(0)
    cap_xd(0)
    cap_y(1)
    cap_y(3)
    img_pair_up(1)
    img_pair_down(1)
    cap_x2(0)
    img_own_up(2)
    img_own_down(2)
    cap_xu(1)
    cap_xd(1)
    cap_y(2)
    img_pair_up(2)
    cap_xu(3)
    cap_xd(3)
    img_pair_down(2)
    img_own_up(3)
    img_own_down(3)
    cap_x2(1)
    cap_xd(2)
    cap_xu(2)
    img_pair_up(3)
    img_pair_down(3)
    cap_x2(3)
    img_own_up(4)
    cap_x2(2)
    img_pair_down(4)
    for dx in range(NX):
        for j in range(NYH):
            got_c(slot_c(j, dx, 1))

    fold = fold_matrix()
    for src, base, dst, off in ((gi, 0, ar, 0), (gc, 0, br, 0), (gc, 256, br, 64)):
        for g, n in ((0, 4), (1, 3)):
            cols = DS + DT + 256 * g
            y = jnp.dot(fold, src[base : base + 256, cols : cols + 256], preferred_element_type=F32).astype(BF)
            for q in range(n):
                c = 256 * (4 * g + q)
                dst[off : off + 64, c : c + 256] = y[64 * q : 64 * q + 64, :]

    row_lse, col_lse, col_max = [], [], []
    for k, (e_row, e_col, lo, width) in enumerate(((es, fs, 0, DS), (et, ft, DS, DT))):
        gain = GAIN / math.sqrt(width)
        cols = slice(lo, lo + width)
        e_col[0:RI, 0:RC] = gain * dot_t(gi[:, cols], gc[:, cols])
        e_col[0:RI, RC:MC] = gain * dot_t(gi[:, cols], br[:, cols])
        e_col[RI:MI, 0:RC] = gain * dot_t(ar[:, cols], gc[:, cols])
        e_col[RI:MI, RC:MC] = gain * dot_t(ar[:, cols], br[:, cols])
        top = None
        lses = []
        for b in range(0, MI, 64):
            blk = e_col[b : b + 64, :]
            m = jnp.max(blk, axis=1, keepdims=True)
            rmx[k, b : b + 64, :] = m
            e = jnp.exp(blk - m)
            e_row[b : b + 64, :] = e
            lses.append(m + jnp.log(jnp.sum(e, axis=1, keepdims=True)))
            t = jnp.max(blk, axis=0, keepdims=True)
            top = t if top is None else jnp.maximum(top, t)
        row_lse.append(lses)
        total = None
        for b in range(0, MI, 64):
            e = jnp.exp(e_col[b : b + 64, :] - top)
            e_col[b : b + 64, :] = e
            t = jnp.sum(e, axis=0, keepdims=True)
            total = t if total is None else total + t
        col_max.append(top)
        col_lse.append(top + jnp.log(total))

    lane = lax.broadcasted_iota(jnp.int32, (64, 128), 1)
    for n, b in enumerate(range(0, MI, 64)):
        tb[b : b + 64, :] = jnp.where(lane == 0, row_lse[0][n], jnp.where(lane == 1, row_lse[1][n], 0.0))
    tb[MI:LI, :] = jnp.zeros((LI - MI, 128), F32)
    me_x = x * 2 + core
    rxc[me_x, 0:1, :] = col_lse[0]
    rxc[me_x, 1:2, :] = col_lse[1]
    peers_x = [(dx, dc) for dx in (2, 1, 3, 0) for dc in (1, 0) if (dx, dc) != (0, 0)]
    for n, (dx, dc) in enumerate(peers_x):
        c = remote(rxc.at[me_x], rxc.at[me_x], lc_s.at[n], lc_r.at[me_x], (at_img(0, dx, dc), cap))
        c.start()
        pending.append(c)
    rxr[z] = tb[...].T[0:2, :]
    peers_z = (4, 3, 5, 2, 6, 1, 7)
    for n, dz in enumerate(peers_z):
        c = remote(rxr.at[z], rxr.at[z], lr_s.at[n], lr_r.at[z], (img, at_cap(0, dz)))
        c.start()
        pending.append(c)

    def pool(parts):
        m = jnp.max(parts, axis=0)
        return m + jnp.log(jnp.sum(jnp.exp(parts - m[None]), axis=0))

    tb2[...] = jnp.zeros_like(tb2)
    for dx, dc in reversed(peers_x):
        s = ((x + dx) % NX) * 2 + (core + dc) % 2
        remote(rxc.at[s], rxc.at[s], lc_s.at[0], lc_r.at[s], up).wait_recv()
    rxc2[yh] = pool(rxc[...])
    for n, d in enumerate((2, 1, 3)):
        c = remote(rxc2.at[yh], rxc2.at[yh], mc_s.at[n], mc_r.at[yh], ys[d - 1])
        c.start()
        pending.append(c)
    for dz in reversed(peers_z):
        s = (z + dz) % NZ
        remote(rxr.at[s], rxr.at[s], lr_s.at[0], lr_r.at[s], up).wait_recv()
    rxr2[yl] = pool(rxr[...])
    c = remote(rxr2.at[yl], rxr2.at[yl], mr_s.at[0], mr_r.at[yl], pair)
    c.start()
    pending.append(c)
    remote(rxr2.at[1 - yl], rxr2.at[1 - yl], mr_s.at[0], mr_r.at[1 - yl], up).wait_recv()
    tb2[0:2, :] = pool(rxr2[...])
    rows_all = tb2[...].T
    for d in (1, 3, 2):
        s = (yh + d) % NYH
        remote(rxc2.at[s], rxc2.at[s], mc_s.at[0], mc_r.at[s], up).wait_recv()
    cols_all = pool(rxc2[...])
    f_col_s = 0.5 * jnp.exp(col_max[0] - cols_all[0:1, :])
    f_col_t = 0.25 * jnp.exp(col_max[1] - cols_all[1:2, :])

    b = lax.broadcasted_iota(jnp.int32, (1, MC), 1)
    t = jnp.where(b < RC, b >> 4, (b - RC) >> 2)
    u = jnp.where(b < RC, b & 15, 16 + (b & 3))
    block = (t & 3) * (2 * NX) + ((t >> 2) & 3) * 2 + (t >> 4)
    col_id = cap * MC + block * B + u
    for lo in range(0, MI, 64):
        a = lo + lax.broadcasted_iota(jnp.int32, (64, 1), 0)
        if lo < RI:
            row_id = img * MI + (a >> 4) * B + (a & 15)
        else:
            row_id = img * MI + ((a - RI) >> 2) * B + 16 + (a & 3)
        rows = slice(lo, lo + 64)
        f_row_s = 0.5 * jnp.exp(rmx[0, rows, :] - rows_all[rows, 0:1])
        f_row_t = 0.25 * jnp.exp(rmx[1, rows, :] - rows_all[rows, 1:2])
        g = es[rows, :] * f_row_s + fs[rows, :] * f_col_s
        g = g - (et[rows, :] * f_row_t + ft[rows, :] * f_col_t)
        g = g - jnp.where(row_id == col_id, 0.5, 0.0)
        tg[rows, :] = g.astype(BF)

    def folded(v):
        v = jnp.concatenate([v[:, 256 * q : 256 * q + 256] for q in range(4)], axis=0)
        hi = v.astype(BF)
        lo = (v - hi.astype(F32)).astype(BF)
        return t_dot(fold, hi) + t_dot(fold, lo)

    pi[...] = jnp.dot(tg[:, 0:RC], gc[:, 0:DS], preferred_element_type=F32) + jnp.dot(
        tg[:, RC:MC], br[:, 0:DS], preferred_element_type=F32
    )
    si[:, 0:DS] = pi[0:RI, :]
    si[:, DS:WG] = folded(pi[RI:MI, :])
    far = (4, 3, 5, 2, 6, 1, 7, 0)
    pair_copies = []
    for n, dz in enumerate(far):
        there = pl.ds(pl.multiple_of(16 * at_cap(1, dz), 16), 16)
        s_p[n] = si[there, :].astype(BF)
        c = remote(s_p.at[n], r_p.at[n], p_s.at[n], p_r.at[n], pair)
        c.start()
        pair_copies.append(c)
        pending.append(c)

    pc[...] = t_dot(tg[0:RI, :], gi[:, 0:DS]) + t_dot(tg[RI:MI, :], ar[:, 0:DS])
    for h in range(2):
        rows = slice(256 * h, 256 * h + 256)
        sc[rows, 0:DS] = pc[rows, :]
        sc[rows, DS:WG] = folded(pc[RC + 64 * h : RC + 64 * h + 64, :])
    half = NX * NYH * 16
    core_copies = []
    for n, dx in enumerate((2, 1, 3, 0)):
        there = pl.ds(pl.multiple_of((1 - core) * half + ((x + dx) % NX) * (NYH * 16), 64), 64)
        c = remote(sc.at[there, :], r_core.at[n], co_s.at[n], co_r.at[n], sib)
        c.start()
        core_copies.append(c)
        pending.append(c)

    def along_z(n):
        dz = far[n]
        here = pl.ds(pl.multiple_of(16 * at_cap(0, dz), 16), 16)
        pair_copies[n].wait_recv()
        v = si[here, :] + r_p[n].astype(F32)
        if dz:
            s_z[n] = v.astype(BF)
            c = remote(s_z.at[n], r_z.at[n], z_s.at[n], z_r.at[n], (img, at_cap(0, dz)))
            c.start()
            pending.append(c)
        return v

    def along_x(n):
        here = pl.ds(pl.multiple_of(core * half + ((x + (2, 1, 3, 0)[n]) % NX) * (NYH * 16), 64), 64)
        core_copies[n].wait_recv()
        v = sc[here, :] + r_core[n]
        if n < 3:
            s_x[n] = v.astype(BF)
            c = remote(s_x.at[n], r_x.at[n], x_s.at[n], x_r.at[n], (x2, xu, xd)[n])
            c.start()
            pending.append(c)
        else:
            s_y[...] = v

    along_z(0)
    along_z(1)
    along_x(0)
    along_z(2)
    along_x(1)
    along_z(3)
    along_x(2)
    along_z(4)
    along_z(5)
    along_z(6)
    along_x(3)
    own_i = along_z(7)

    v = s_y[...]
    for n in (1, 2, 0):
        remote(r_x.at[n], r_x.at[n], x_s.at[n], x_r.at[n], up).wait_recv()
        v = v + r_x[n].astype(F32)
    s_y[...] = v
    for n, d in enumerate((2, 1, 3)):
        there = pl.ds(pl.multiple_of(16 * ((yh + d) % NYH), 16), 16)
        s_x[3, 16 * n : 16 * n + 16, :] = s_y[there, :].astype(BF)
        c = remote(s_x.at[3, pl.ds(16 * n, 16), :], r_y.at[n], y_s.at[n], y_r.at[n], ys[d - 1])
        c.start()
        pending.append(c)

    def unfold(acc, out):
        out[0:16, :] = acc[:, 0:DS]
        for q in range(4):
            out[16:20, 256 * q : 256 * q + 256] = acc[4 * q : 4 * q + 4, DS:WG]

    acc = own_i
    for n in reversed(range(NZ - 1)):
        remote(r_z.at[n], r_z.at[n], z_s.at[n], z_r.at[n], up).wait_recv()
        acc = acc + r_z[n].astype(F32)
    unfold(acc, oi_ref)

    acc = s_y[pl.ds(pl.multiple_of(16 * yh, 16), 16), :]
    for n in range(3):
        remote(r_y.at[n], r_y.at[n], y_s.at[n], y_r.at[n], up).wait_recv()
        acc = acc + r_y[n].astype(F32)
    unfold(acc, oc_ref)

    for c in pending:
        c.wait_send()


def local(image_student, caption_student, image_teacher, caption_teacher):
    vmem = pl.BlockSpec(memory_space=pltpu.VMEM)
    dma = pltpu.SemaphoreType.DMA
    out = jax.ShapeDtypeStruct((B, DS), F32)
    return pl.pallas_call(
        kernel,
        out_shape=(out, out),
        in_specs=[pl.BlockSpec(memory_space=pltpu.HBM)] * 4,
        out_specs=(vmem, vmem),
        scratch_shapes=[
            pltpu.VMEM((B, DS), BF),
            pltpu.VMEM((B, DS), BF),
            pltpu.VMEM((B, DT), BF),
            pltpu.VMEM((B, DT), BF),
            pltpu.VMEM((RI, W), BF),
            pltpu.VMEM((RC, W), BF),
            pltpu.VMEM((MI - RI, DS + DT), BF),
            pltpu.VMEM((MC - RC, DS + DT), BF),
            pltpu.VMEM((16, 512), F32),
            pltpu.VMEM((MI, MC), F32),
            pltpu.VMEM((MI, MC), F32),
            pltpu.VMEM((MI, MC), F32),
            pltpu.VMEM((MI, MC), F32),
            pltpu.VMEM((2, MI, 1), F32),
            pltpu.VMEM((LI, 128), F32),
            pltpu.VMEM((128, LI), F32),
            pltpu.VMEM((NZ, 2, LI), F32),
            pltpu.VMEM((2 * NX, 2, MC), F32),
            pltpu.VMEM((2, 2, LI), F32),
            pltpu.VMEM((NYH, 2, MC), F32),
            pltpu.VMEM((MI, MC), BF),
            pltpu.VMEM((MI, DS), F32),
            pltpu.VMEM((RI, WG), F32),
            pltpu.VMEM((NZ, 16, WG), BF),
            pltpu.VMEM((NZ, 16, WG), BF),
            pltpu.VMEM((NZ - 1, 16, WG), BF),
            pltpu.VMEM((NZ - 1, 16, WG), BF),
            pltpu.VMEM((MC, DS), F32),
            pltpu.VMEM((RC, WG), F32),
            pltpu.VMEM((4, 64, WG), F32),
            pltpu.VMEM((4, 64, WG), BF),
            pltpu.VMEM((3, 64, WG), BF),
            pltpu.VMEM((64, WG), F32),
            pltpu.VMEM((3, 16, WG), BF),
            dma((4,)),
            dma((NI,)), dma((15,)), dma((NC,)), dma((31,)),
            dma((8,)), dma((7,)), dma((8,)), dma((7,)),
            dma((2,)), dma((1,)), dma((4,)), dma((3,)),
            dma((8,)), dma((8,)), dma((7,)), dma((7,)),
            dma((4,)), dma((4,)), dma((3,)), dma((3,)), dma((3,)), dma((3,)),
        ],
        compiler_params=pltpu.CompilerParams(
            collective_id=0, has_side_effects=True, vmem_limit_bytes=63 * 2**20
        ),
        cost_estimate=pl.CostEstimate(flops=1_600_000_000, bytes_accessed=400_000, transcendentals=900_000),
        name="contrastive",
    )(image_student, caption_student, image_teacher, caption_teacher)


def solution(mesh):
    return jax.shard_map(
        local,
        mesh=mesh,
        in_specs=(
            P(("img", "cap"), None),
            P(("cap", "img"), None),
            P(("img", "cap"), None),
            P(("cap", "img"), None),
        ),
        out_specs=(P(("img", "cap"), None), P(("cap", "img"), None)),
        check_vma=False,
    )
```

```python
import math

import jax
import jax.numpy as jnp
from jax import lax
from jax.experimental import pallas as pl
from jax.experimental.pallas import tpu as pltpu
from jax.sharding import PartitionSpec as P

MESH = pl.DeviceIdType.MESH
GAIN = 3.0
NX, NYH, NZ = 4, 4, 8
NI, NC = 2 * NZ, 2 * NX * NYH
DS, DT = 1024, 768
W = DS + DT + 512
WG = DS + 256
B = 20
RI, RC = 16 * NI, 16 * NC
MI, MC = 20 * NI, 20 * NC
LI = 384
BF, F32 = jnp.bfloat16, jnp.float32


def dot_t(a, b):
    return lax.dot_general(a, b, (((1,), (1,)), ((), ())), preferred_element_type=F32)


def t_dot(a, b):
    return lax.dot_general(a, b, (((0,), (0,)), ((), ())), preferred_element_type=F32)


def fold_matrix():
    a = lax.broadcasted_iota(jnp.int32, (256, 256), 0)
    b = lax.broadcasted_iota(jnp.int32, (256, 256), 1)
    source = 16 * ((a >> 2) & 15) + 4 * (a >> 6) + (a & 3)
    return jnp.where(b == source, 1.0, 0.0).astype(BF)


def kernel(
    is_hbm, cs_hbm, it_hbm, ct_hbm, oi_ref, oc_ref,
    is_ref, cs_ref, it_ref, ct_ref,
    gi, gc, ar, br, rp, es, et, fs, ft, rmx, tb, tb2, rxr, rxk, rxc,
    tg, pi, si, s_p, r_p, s_z, r_z, pc, sc, r_core, s_v, s_x, r_x, s_y, r_y,
    in_sem, gi_r, gi_s, gc_r, gc_s, lr_r, lr_s, lk_r, lk_s, lc_r, lc_s,
    p_r, p_s, z_r, z_s, co_r, co_s, x_r, x_s, y_r, y_s,
):
    img, cap = lax.axis_index("img"), lax.axis_index("cap")
    yh, x, core = img // (2 * NX), (img // 2) % NX, img % 2
    yl, z = cap // NZ, cap % NZ

    def at_img(dyh, dx, dcore):
        return (((yh + dyh) % NYH) * NX + (x + dx) % NX) * 2 + (core + dcore) % 2

    def slot_c(dyh, dx, dcore):
        return ((core + dcore) % 2) * (NX * NYH) + ((yh + dyh) % NYH) * NX + (x + dx) % NX

    def at_cap(dyl, dz):
        return ((yl + dyl) % 2) * NZ + (z + dz) % NZ

    def remote(src, dst, send, recv, dev):
        return pltpu.make_async_remote_copy(
            src_ref=src, dst_ref=dst, send_sem=send, recv_sem=recv, device_id=dev, device_id_type=MESH
        )

    up, down, pair = (img, at_cap(0, 1)), (img, at_cap(0, -1)), (img, at_cap(1, 0))
    xu, xd, x2 = (at_img(0, 1, 0), cap), (at_img(0, -1, 0), cap), (at_img(0, 2, 0), cap)
    sib = (at_img(0, 0, 1), cap)
    ys = [(at_img(d, 0, 0), cap) for d in (1, 2, 3)]

    barrier = pltpu.get_barrier_semaphore()
    near = [up, down, pair, xu, xd, x2, sib] + ys
    for dev in near:
        pl.semaphore_signal(barrier, inc=1, device_id=dev, device_id_type=MESH)

    loads = []
    for n, (src, dst) in enumerate(((is_hbm, is_ref), (cs_hbm, cs_ref), (it_hbm, it_ref), (ct_hbm, ct_ref))):
        c = pltpu.make_async_copy(src, dst, in_sem.at[n])
        c.start()
        loads.append(c)
    for c in loads:
        c.wait()

    me_i, me_c = cap, slot_c(0, 0, 0)
    for s_ref, t_ref, buf, slot in ((is_ref, it_ref, gi, me_i), (cs_ref, ct_ref, gc, me_c)):
        rows = pl.ds(pl.multiple_of(16 * slot, 16), 16)
        buf[rows, 0:DS] = s_ref[0:16, :]
        buf[rows, DS : DS + DT] = t_ref[0:16, :]
        s4 = s_ref[...].astype(F32)[16:20, :]
        t4 = t_ref[...].astype(F32)[16:20, :]
        rp[...] = jnp.zeros_like(rp)
        for q in range(4):
            rp[4 * q : 4 * q + 4, 0:256] = s4[:, 256 * q : 256 * q + 256]
        for q in range(3):
            rp[4 * q : 4 * q + 4, 256:512] = t4[:, 256 * q : 256 * q + 256]
        buf[rows, DS + DT : W] = rp[...].astype(BF)

    pl.semaphore_wait(barrier, len(near))

    pending = []

    def gi_at(slot):
        return gi.at[pl.ds(pl.multiple_of(16 * slot, 16), 16), :]

    def gc_at(slot):
        return gc.at[pl.ds(pl.multiple_of(16 * slot, 16), 16), :]

    count = {"i": 0, "c": 0}

    def send_i(slot, *devs):
        for dev in devs:
            c = remote(gi_at(slot), gi_at(slot), gi_s.at[count["i"]], gi_r.at[slot], dev)
            count["i"] += 1
            c.start()
            pending.append(c)

    def send_c(slot, *devs):
        for dev in devs:
            c = remote(gc_at(slot), gc_at(slot), gc_s.at[count["c"]], gc_r.at[slot], dev)
            count["c"] += 1
            c.start()
            pending.append(c)

    def got_i(slot):
        remote(gi_at(slot), gi_at(slot), gi_s.at[0], gi_r.at[slot], up).wait_recv()

    def got_c(slot):
        remote(gc_at(slot), gc_at(slot), gc_s.at[0], gc_r.at[slot], up).wait_recv()

    def img_own_up(k):
        s = at_cap(0, -k)
        got_i(s)
        if k < 4:
            send_i(s, up)

    def img_own_down(k):
        s = at_cap(0, k)
        got_i(s)
        if k < 3:
            send_i(s, down)

    def img_pair_up(k):
        s = at_cap(1, -k)
        got_i(s)
        if k < 3:
            send_i(s, up)

    def img_pair_down(k):
        s = at_cap(1, k)
        got_i(s)
        if k < 4:
            send_i(s, down)

    def cap_y(j):
        s = slot_c(j, 0, 0)
        got_c(s)
        send_c(s, xu, xd, sib)

    def cap_xu(j):
        s = slot_c(j, -1, 0)
        got_c(s)
        if j < 2:
            send_c(s, xu)
        send_c(s, sib)

    def cap_xd(j):
        s = slot_c(j, 1, 0)
        got_c(s)
        if j >= 2:
            send_c(s, xd)
        send_c(s, sib)

    def cap_x2(j):
        s = slot_c(j, 2, 0)
        got_c(s)
        send_c(s, sib)

    send_i(me_i, pair)
    send_c(me_c, *ys)
    send_i(me_i, up, down)
    send_c(me_c, xu, xd, sib)

    s = at_cap(1, 0)
    got_i(s)
    send_i(s, up, down)
    img_own_up(1)
    img_own_down(1)
    cap_xu(0)
    cap_xd(0)
    cap_y(1)
    cap_y(3)
    img_pair_up(1)
    img_pair_down(1)
    cap_x2(0)
    img_own_up(2)
    img_own_down(2)
    cap_xu(1)
    cap_xd(1)
    cap_y(2)
    img_pair_up(2)
    cap_xu(3)
    cap_xd(3)
    img_pair_down(2)
    img_own_up(3)
    img_own_down(3)
    cap_x2(1)
    cap_xd(2)
    cap_xu(2)
    img_pair_up(3)
    img_pair_down(3)
    cap_x2(3)
    img_own_up(4)
    cap_x2(2)
    img_pair_down(4)
    for dx in range(NX):
        for j in range(NYH):
            got_c(slot_c(j, dx, 1))

    fold = fold_matrix()
    for src, base, dst, off in ((gi, 0, ar, 0), (gc, 0, br, 0), (gc, 256, br, 64)):
        for g, n in ((0, 4), (1, 3)):
            cols = DS + DT + 256 * g
            y = jnp.dot(fold, src[base : base + 256, cols : cols + 256], preferred_element_type=F32).astype(BF)
            for q in range(n):
                c = 256 * (4 * g + q)
                dst[off : off + 64, c : c + 256] = y[64 * q : 64 * q + 64, :]

    row_lse, col_lse, col_max = [], [], []
    for k, (e_row, e_col, lo, width) in enumerate(((es, fs, 0, DS), (et, ft, DS, DT))):
        gain = GAIN / math.sqrt(width)
        cols = slice(lo, lo + width)
        e_col[0:RI, 0:RC] = gain * dot_t(gi[:, cols], gc[:, cols])
        e_col[0:RI, RC:MC] = gain * dot_t(gi[:, cols], br[:, cols])
        e_col[RI:MI, 0:RC] = gain * dot_t(ar[:, cols], gc[:, cols])
        e_col[RI:MI, RC:MC] = gain * dot_t(ar[:, cols], br[:, cols])
        top = None
        lses = []
        for b in range(0, MI, 64):
            blk = e_col[b : b + 64, :]
            m = jnp.max(blk, axis=1, keepdims=True)
            rmx[k, b : b + 64, :] = m
            e = jnp.exp(blk - m)
            e_row[b : b + 64, :] = e
            lses.append(m + jnp.log(jnp.sum(e, axis=1, keepdims=True)))
            t = jnp.max(blk, axis=0, keepdims=True)
            top = t if top is None else jnp.maximum(top, t)
        row_lse.append(lses)
        total = None
        for b in range(0, MI, 64):
            e = jnp.exp(e_col[b : b + 64, :] - top)
            e_col[b : b + 64, :] = e
            t = jnp.sum(e, axis=0, keepdims=True)
            total = t if total is None else total + t
        col_max.append(top)
        col_lse.append(top + jnp.log(total))

    lane = lax.broadcasted_iota(jnp.int32, (64, 128), 1)
    for n, b in enumerate(range(0, MI, 64)):
        tb[b : b + 64, :] = jnp.where(lane == 0, row_lse[0][n], jnp.where(lane == 1, row_lse[1][n], 0.0))
    tb[MI:LI, :] = jnp.zeros((LI - MI, 128), F32)
    rxk[core, 0:1, :] = col_lse[0]
    rxk[core, 1:2, :] = col_lse[1]
    c = remote(rxk.at[core], rxk.at[core], lk_s.at[0], lk_r.at[core], sib)
    c.start()
    pending.append(c)
    rxr[me_i] = tb[...].T[0:2, :]
    peers_r = [(dy, dz) for dz in (4, 3, 5, 2, 6, 1, 7, 0) for dy in (1, 0) if (dy, dz) != (0, 0)]
    for n, (dy, dz) in enumerate(peers_r):
        c = remote(rxr.at[me_i], rxr.at[me_i], lr_s.at[n], lr_r.at[me_i], (img, at_cap(dy, dz)))
        c.start()
        pending.append(c)

    def pool(parts):
        m = jnp.max(parts, axis=0)
        return m + jnp.log(jnp.sum(jnp.exp(parts - m[None]), axis=0))

    tb2[...] = jnp.zeros_like(tb2)
    remote(rxk.at[1 - core], rxk.at[1 - core], lk_s.at[0], lk_r.at[1 - core], up).wait_recv()
    me_x = yh * NX + x
    rxc[me_x] = pool(rxk[...])
    peers_c = [(j, dx) for j in (2, 1, 3, 0) for dx in (2, 1, 3, 0) if (j, dx) != (0, 0)]
    for n, (j, dx) in enumerate(peers_c):
        c = remote(rxc.at[me_x], rxc.at[me_x], lc_s.at[n], lc_r.at[me_x], (at_img(j, dx, 0), cap))
        c.start()
        pending.append(c)
    for dy, dz in reversed(peers_r):
        s = at_cap(dy, dz)
        remote(rxr.at[s], rxr.at[s], lr_s.at[0], lr_r.at[s], up).wait_recv()
    tb2[0:2, :] = pool(rxr[...])
    rows_all = tb2[...].T
    for j, dx in reversed(peers_c):
        s = ((yh + j) % NYH) * NX + (x + dx) % NX
        remote(rxc.at[s], rxc.at[s], lc_s.at[0], lc_r.at[s], up).wait_recv()
    cols_all = pool(rxc[...])
    f_col_s = 0.5 * jnp.exp(col_max[0] - cols_all[0:1, :])
    f_col_t = 0.25 * jnp.exp(col_max[1] - cols_all[1:2, :])

    b = lax.broadcasted_iota(jnp.int32, (1, MC), 1)
    t = jnp.where(b < RC, b >> 4, (b - RC) >> 2)
    u = jnp.where(b < RC, b & 15, 16 + (b & 3))
    block = (t >> 2 & 3) * (2 * NX) + (t & 3) * 2 + (t >> 4)
    col_id = cap * MC + block * B + u
    for lo in range(0, MI, 64):
        a = lo + lax.broadcasted_iota(jnp.int32, (64, 1), 0)
        if lo < RI:
            row_id = img * MI + (a >> 4) * B + (a & 15)
        else:
            row_id = img * MI + ((a - RI) >> 2) * B + 16 + (a & 3)
        rows = slice(lo, lo + 64)
        f_row_s = 0.5 * jnp.exp(rmx[0, rows, :] - rows_all[rows, 0:1])
        f_row_t = 0.25 * jnp.exp(rmx[1, rows, :] - rows_all[rows, 1:2])
        g = es[rows, :] * f_row_s + fs[rows, :] * f_col_s
        g = g - (et[rows, :] * f_row_t + ft[rows, :] * f_col_t)
        g = g - jnp.where(row_id == col_id, 0.5, 0.0)
        tg[rows, :] = g.astype(BF)

    def folded(v):
        v = jnp.concatenate([v[:, 256 * q : 256 * q + 256] for q in range(4)], axis=0)
        hi = v.astype(BF)
        lo = (v - hi.astype(F32)).astype(BF)
        return t_dot(fold, hi) + t_dot(fold, lo)

    pc[...] = t_dot(tg[0:RI, :], gi[:, 0:DS]) + t_dot(tg[RI:MI, :], ar[:, 0:DS])
    for h in range(2):
        rows = slice(256 * h, 256 * h + 256)
        sc[rows, 0:DS] = pc[rows, :]
        sc[rows, DS:WG] = folded(pc[RC + 64 * h : RC + 64 * h + 64, :])
    group = NX * 16

    def group_at(dcore, d):
        at = ((core + dcore) % 2) * NYH + (yh + d) % NYH
        return pl.ds(pl.multiple_of(group * at, group), group)

    order_y = (2, 1, 3, 0)
    core_copies = []
    for n, d in enumerate(order_y):
        c = remote(sc.at[group_at(1, d), :], r_core.at[n], co_s.at[n], co_r.at[n], sib)
        c.start()
        core_copies.append(c)
        pending.append(c)

    pi[...] = jnp.dot(tg[:, 0:RC], gc[:, 0:DS], preferred_element_type=F32) + jnp.dot(
        tg[:, RC:MC], br[:, 0:DS], preferred_element_type=F32
    )
    si[:, 0:DS] = pi[0:RI, :]
    si[:, DS:WG] = folded(pi[RI:MI, :])
    far = (4, 3, 5, 2, 6, 1, 7, 0)
    pair_copies = []
    for n, dz in enumerate(far):
        there = pl.ds(pl.multiple_of(16 * at_cap(1, dz), 16), 16)
        s_p[n] = si[there, :].astype(BF)
        c = remote(s_p.at[n], r_p.at[n], p_s.at[n], p_r.at[n], pair)
        c.start()
        pair_copies.append(c)
        pending.append(c)

    def along_z(n):
        dz = far[n]
        here = pl.ds(pl.multiple_of(16 * at_cap(0, dz), 16), 16)
        pair_copies[n].wait_recv()
        v = si[here, :] + r_p[n].astype(F32)
        if dz:
            s_z[n] = v.astype(BF)
            c = remote(s_z.at[n], r_z.at[n], z_s.at[n], z_r.at[n], (img, at_cap(0, dz)))
            c.start()
            pending.append(c)
        return v

    def along_x(n):
        core_copies[n].wait_recv()
        v = sc[group_at(0, order_y[n]), :] + r_core[n]
        s_v[n] = v
        s_x[n] = v.astype(BF)
        for k, (dx, dev) in enumerate(((2, x2), (1, xu), (3, xd))):
            there = pl.ds(pl.multiple_of(16 * ((x + dx) % NX), 16), 16)
            m = 3 * n + k
            c = remote(s_x.at[n, there, :], r_x.at[m], x_s.at[m], x_r.at[m], dev)
            c.start()
            pending.append(c)

    def along_y(n):
        v = s_v[n, pl.ds(pl.multiple_of(16 * x, 16), 16), :]
        for k in (1, 2, 0):
            m = 3 * n + k
            remote(r_x.at[m], r_x.at[m], x_s.at[m], x_r.at[m], up).wait_recv()
            v = v + r_x[m].astype(F32)
        if n < 3:
            s_y[n] = v.astype(BF)
            c = remote(s_y.at[n], r_y.at[n], y_s.at[n], y_r.at[n], ys[order_y[n] - 1])
            c.start()
            pending.append(c)
        return v

    along_x(0)
    along_x(1)
    along_z(0)
    along_x(2)
    along_z(1)
    along_x(3)
    along_z(2)
    along_y(0)
    along_z(3)
    along_y(1)
    along_z(4)
    along_z(5)
    along_y(2)
    along_z(6)
    own_i = along_z(7)
    own_c = along_y(3)

    def unfold(acc, out):
        out[0:16, :] = acc[:, 0:DS]
        for q in range(4):
            out[16:20, 256 * q : 256 * q + 256] = acc[4 * q : 4 * q + 4, DS:WG]

    acc = own_i
    for n in reversed(range(NZ - 1)):
        remote(r_z.at[n], r_z.at[n], z_s.at[n], z_r.at[n], up).wait_recv()
        acc = acc + r_z[n].astype(F32)
    unfold(acc, oi_ref)

    acc = own_c
    for n in (1, 2, 0):
        remote(r_y.at[n], r_y.at[n], y_s.at[n], y_r.at[n], up).wait_recv()
        acc = acc + r_y[n].astype(F32)
    unfold(acc, oc_ref)

    for c in pending:
        c.wait_send()


def local(image_student, caption_student, image_teacher, caption_teacher):
    vmem = pl.BlockSpec(memory_space=pltpu.VMEM)
    dma = pltpu.SemaphoreType.DMA
    out = pltpu.VMEM((B, DS), F32)
    return pl.pallas_call(
        kernel,
        out_shape=(out, out),
        in_specs=[pl.BlockSpec(memory_space=pltpu.HBM)] * 4,
        out_specs=(vmem, vmem),
        scratch_shapes=[
            pltpu.VMEM((B, DS), BF),
            pltpu.VMEM((B, DS), BF),
            pltpu.VMEM((B, DT), BF),
            pltpu.VMEM((B, DT), BF),
            pltpu.VMEM((RI, W), BF),
            pltpu.VMEM((RC, W), BF),
            pltpu.VMEM((MI - RI, DS + DT), BF),
            pltpu.VMEM((MC - RC, DS + DT), BF),
            pltpu.VMEM((16, 512), F32),
            pltpu.VMEM((MI, MC), F32),
            pltpu.VMEM((MI, MC), F32),
            pltpu.VMEM((MI, MC), F32),
            pltpu.VMEM((MI, MC), F32),
            pltpu.VMEM((2, MI, 1), F32),
            pltpu.VMEM((LI, 128), F32),
            pltpu.VMEM((128, LI), F32),
            pltpu.VMEM((NI, 2, LI), F32),
            pltpu.VMEM((2, 2, MC), F32),
            pltpu.VMEM((NX * NYH, 2, MC), F32),
            pltpu.VMEM((MI, MC), BF),
            pltpu.VMEM((MI, DS), F32),
            pltpu.VMEM((RI, WG), F32),
            pltpu.VMEM((NZ, 16, WG), BF),
            pltpu.VMEM((NZ, 16, WG), BF),
            pltpu.VMEM((NZ - 1, 16, WG), BF),
            pltpu.VMEM((NZ - 1, 16, WG), BF),
            pltpu.VMEM((MC, DS), F32),
            pltpu.VMEM((RC, WG), F32),
            pltpu.VMEM((4, 64, WG), F32),
            pltpu.VMEM((4, 64, WG), F32),
            pltpu.VMEM((4, 64, WG), BF),
            pltpu.VMEM((12, 16, WG), BF),
            pltpu.VMEM((3, 16, WG), BF),
            pltpu.VMEM((3, 16, WG), BF),
            dma((4,)),
            dma((NI,)), dma((15,)), dma((NC,)), dma((31,)),
            dma((NI,)), dma((15,)), dma((2,)), dma((1,)), dma((16,)), dma((15,)),
            dma((8,)), dma((8,)), dma((7,)), dma((7,)),
            dma((4,)), dma((4,)), dma((12,)), dma((12,)), dma((3,)), dma((3,)),
        ],
        compiler_params=pltpu.CompilerParams(
            collective_id=0, has_side_effects=True, vmem_limit_bytes=56 * 2**20
        ),
        cost_estimate=pl.CostEstimate(flops=1_600_000_000, bytes_accessed=400_000, transcendentals=900_000),
        name="contrastive",
    )(*(pltpu.with_memory_space_constraint(a, pltpu.HBM) for a in (image_student, caption_student, image_teacher, caption_teacher)))


def solution(mesh):
    return jax.shard_map(
        local,
        mesh=mesh,
        in_specs=(
            P(("img", "cap"), None),
            P(("cap", "img"), None),
            P(("img", "cap"), None),
            P(("cap", "img"), None),
        ),
        out_specs=(P(("img", "cap"), None), P(("cap", "img"), None)),
        check_vma=False,
    )
```

```python
import math

import jax
import jax.numpy as jnp
from jax import lax
from jax.experimental import pallas as pl
from jax.experimental.pallas import tpu as pltpu
from jax.sharding import PartitionSpec as P

MESH = pl.DeviceIdType.MESH
GAIN = 3.0
NX, NYH, NZ = 4, 4, 8
NR = NQ = 16
DS, DT = 1024, 768
W = 256 + DS
WIDTH = (256 + DS, 256 + DT)
B = 20
MAIN, M = 32 * NR, 40 * NR
BF, F32 = jnp.bfloat16, jnp.float32
ORDER = "P0U1D1L0R0Y1Y3E1F1X0U2D2L1R1Y2E2L3R3F2U3D3X1R2L2E3F3X3U4X2F4"


def dot_t(a, b):
    return lax.dot_general(a, b, (((1,), (1,)), ((), ())), preferred_element_type=F32)


def t_dot(a, b):
    return lax.dot_general(a, b, (((0,), (0,)), ((), ())), preferred_element_type=F32)


def dot(a, b):
    return jnp.dot(a, b, preferred_element_type=F32)


def fold_matrix():
    a = lax.broadcasted_iota(jnp.int32, (256, 256), 0)
    b = lax.broadcasted_iota(jnp.int32, (256, 256), 1)
    source = 16 * ((a >> 2) & 15) + 4 * (a >> 6) + (a & 3)
    return jnp.where(b == source, 1.0, 0.0).astype(BF)


def pool(parts):
    m = jnp.max(parts, axis=0)
    return m + jnp.log(jnp.sum(jnp.exp(parts - m[None]), axis=0))


def kernel(
    is_hbm, cs_hbm, it_hbm, ct_hbm, oi_ref, oc_ref,
    is_ref, cs_ref, it_ref, ct_ref, rp, pk, gi, gc, ar, br, gcs, brs,
    sb, er, ec, rmx, cmx, tb, tb2, rxr, rxc, tg,
    pg, sg, s_p, r_p, s_z, r_z, s_x, r_x, s_y, r_y, own_i, own_c, o_s,
    in_sem, sib_r, sib_s, gi_r, gc_r, first_s, next_s, ex_r, ex_s, lr_r, lr_s, lc_r, lc_s,
    p_r, p_s, z_r, z_s, x_r, x_s, y_r, y_s, o_r, o_send,
):
    img, cap = lax.axis_index("img"), lax.axis_index("cap")
    yh, x, core = img // (2 * NX), (img // 2) % NX, img % 2
    yl, z = cap // NZ, cap % NZ

    def at_img(dyh, dx):
        return (((yh + dyh) % NYH) * NX + (x + dx) % NX) * 2

    def slot_c(dyh, dx):
        return ((yh + dyh) % NYH) * NX + (x + dx) % NX

    def at_cap(dyl, dz):
        return ((yl + dyl) % 2) * NZ + (z + dz) % NZ

    def rows(slot, n):
        return pl.ds(pl.multiple_of(n * slot, n), n)

    def remote(src, dst, send, recv, dev):
        return pltpu.make_async_remote_copy(
            src_ref=src, dst_ref=dst, send_sem=send, recv_sem=recv, device_id=dev, device_id_type=MESH
        )

    def push(src, dst, send, recv, dev):
        remote(src, dst, send, recv, dev).start()

    def sent(ref, sem):
        remote(ref, ref, sem, in_sem.at[0], sib).wait_send()

    up, down, pair = (img, at_cap(0, 1)), (img, at_cap(0, -1)), (img, at_cap(1, 0))
    xu, xd, x2 = [(at_img(0, d) + core, cap) for d in (1, -1, 2)]
    ys = [(at_img(d, 0) + core, cap) for d in (1, 2, 3)]
    sib = (at_img(0, 0) + 1 - core, cap)

    def arrived(ref, sem):
        remote(ref, ref, in_sem.at[0], sem, sib).wait_recv()

    barrier = pltpu.get_barrier_semaphore()
    chip = at_img(0, 0)
    around_i = [(chip, at_cap(1, 0)), (chip, at_cap(0, 1)), (chip, at_cap(0, -1))]
    around_c = [(at_img(*d), cap) for d in ((2, 0), (1, 0), (3, 0), (0, 1), (0, -1))]
    near = [sib] + [(dev[0] + c, dev[1]) for dev in around_i + around_c for c in range(2)]
    for dev in near:
        pl.semaphore_signal(barrier, inc=1, device_id=dev, device_id_type=MESH)

    loads = []
    for n, (src, dst) in enumerate(((is_hbm, is_ref), (it_hbm, it_ref), (cs_hbm, cs_ref), (ct_hbm, ct_ref))):
        c = pltpu.make_async_copy(src, dst, in_sem.at[n])
        c.start()
        loads.append(c)
    for c in loads:
        c.wait()

    for n, (k, j, src, width) in enumerate(
        ((0, 0, is_ref, DS), (1, 0, it_ref, DT), (0, 1, cs_ref, DS), (1, 1, ct_ref, DT))
    ):
        pk[k, j, :, 256 : 256 + width] = src[0:16, :]
        if width < DS:
            pk[k, j, :, 256 + width : W] = jnp.zeros((16, DS - width), BF)
        last = src[...].astype(F32)[16:20, :]
        rp[n] = jnp.zeros((16, 256), F32)
        for q in range(width // 256):
            rp[n, 4 * q : 4 * q + 4, :] = last[:, 256 * q : 256 * q + 256]
        pk[k, j, :, 0:256] = rp[n].astype(BF)

    @pl.when(core == 1)
    def _():
        gi[:, 256 + DT : W] = jnp.zeros((MAIN, DS - DT), BF)
        gc[:, 256 + DT : W] = jnp.zeros((MAIN, DS - DT), BF)

    pl.semaphore_wait(barrier, len(near))

    me_i, me_c = cap, slot_c(0, 0)
    mine_i, mine_c = rows(2 * me_i + core, 16), rows(2 * me_c + core, 16)
    for k, width in enumerate(WIDTH):

        @pl.when(core != k)
        def _():
            w = pl.ds(0, width)
            push(pk.at[k, 0, :, w], gi.at[mine_i, w], sib_s.at[0], sib_r.at[0], sib)
            push(pk.at[k, 1, :, w], gc.at[mine_c, w], sib_s.at[1], sib_r.at[1], sib)

    for dev in around_i:
        for k, width in enumerate(WIDTH):
            w = pl.ds(0, width)
            push(pk.at[k, 0, :, w], gi.at[mine_i, w], first_s.at[k], gi_r.at[me_i], (dev[0] + k, dev[1]))
    for dev in around_c:
        for k, width in enumerate(WIDTH):
            w = pl.ds(0, width)
            push(pk.at[k, 1, :, w], gc.at[mine_c, w], first_s.at[k], gc_r.at[me_c], (dev[0] + k, dev[1]))
    gi[mine_i, :] = pk[core, 0]
    gc[mine_c, :] = pk[core, 1]

    flow = {}
    for k in (1, 2, 3):
        flow["U%d" % k] = (at_cap(0, -k), (up,))
        flow["D%d" % k] = (at_cap(0, k), (down,) if k < 3 else ())
        flow["E%d" % k] = (at_cap(1, -k), (up,) if k < 3 else ())
        flow["F%d" % k] = (at_cap(1, k), (down,))
    flow["P0"] = (at_cap(1, 0), (up, down))
    flow["U4"] = (at_cap(0, -4), ())
    flow["F4"] = (at_cap(1, 4), ())
    for j in range(NYH):
        if j:
            flow["Y%d" % j] = (slot_c(j, 0), (xu, xd))
        flow["L%d" % j] = (slot_c(j, -1), (xu,) if j < 2 else ())
        flow["R%d" % j] = (slot_c(j, 1), (xd,) if j >= 2 else ())
        flow["X%d" % j] = (slot_c(j, 2), ())

    for k, width in enumerate(WIDTH):

        @pl.when(core == k)
        def _():
            for n in range(0, len(ORDER), 2):
                name = ORDER[n : n + 2]
                slot, devs = flow[name]
                buf, recv, send = (gc, gc_r, next_s.at[1]) if name[0] in "YLRX" else (gi, gi_r, next_s.at[0])
                block = buf.at[rows(slot, 32), pl.ds(0, width)]
                arrived(block, recv.at[slot])
                for dev in devs:
                    push(block, block, send, recv.at[slot], dev)
            arrived(gi.at[rows(2 * me_i + 1 - core, 16), pl.ds(0, width)], sib_r.at[0])
            arrived(gc.at[rows(2 * me_c + 1 - core, 16), pl.ds(0, width)], sib_r.at[1])

    @pl.when(core == 0)
    def _():
        push(gc.at[:, pl.ds(256, DS)], gcs, ex_s.at[1], ex_r.at[1], sib)

    fold = fold_matrix()
    for src, dst in ((gi, ar), (gc, br)):
        for h in range(2):
            y = dot(fold, src[256 * h : 256 * h + 256, 0:256]).astype(BF)
            for q in range(4):
                dst[64 * h : 64 * h + 64, 256 * q : 256 * q + 256] = y[64 * q : 64 * q + 64, :]

    @pl.when(core == 0)
    def _():
        push(br, brs, ex_s.at[2], ex_r.at[2], sib)

    gain = jnp.where(core == 0, GAIN / math.sqrt(DS), GAIN / math.sqrt(DT))
    sb[core, 0:MAIN, 0:MAIN] = gain * dot_t(gi[:, 256:W], gc[:, 256:W])
    sb[core, 0:MAIN, MAIN:M] = gain * dot_t(gi[:, 256:W], br[...])
    sb[core, MAIN:M, 0:MAIN] = gain * dot_t(ar[...], gc[:, 256:W])
    sb[core, MAIN:M, MAIN:M] = gain * dot_t(ar[...], br[...])
    push(sb.at[core], sb.at[core], ex_s.at[0], ex_r.at[0], sib)

    def statistics(k):
        top, total, lses = None, None, []
        for b in range(0, M, 64):
            blk = sb[k, b : b + 64, :]
            m = jnp.max(blk, axis=1, keepdims=True)
            rmx[k, b : b + 64, :] = m
            e = jnp.exp(blk - m)
            er[k, b : b + 64, :] = e
            lses.append(m + jnp.log(jnp.sum(e, axis=1, keepdims=True)))
            t = jnp.max(blk, axis=0, keepdims=True)
            top = t if top is None else jnp.maximum(top, t)
        for b in range(0, M, 64):
            e = jnp.exp(sb[k, b : b + 64, :] - top)
            ec[k, b : b + 64, :] = e
            t = jnp.sum(e, axis=0, keepdims=True)
            total = t if total is None else total + t
        cmx[k] = top
        return lses, top + jnp.log(total)

    row_lse, col_lse = statistics(core)

    rxc[core * NQ + me_c] = col_lse
    for n, b in enumerate(range(0, M, 64)):
        tb[b : b + 64, :] = jnp.broadcast_to(row_lse[n], (64, 128))
    rxr[core * NR + me_i] = tb[...].T[0:1, :]
    mine = rxc.at[core * NQ + me_c]
    for j in (2, 1, 3, 0):
        for dx in (2, 1, 3, 0):
            if (j, dx) != (0, 0):
                for c in range(2):
                    push(mine, mine, lc_s.at[0], lc_r.at[core], (at_img(j, dx) + c, cap))
    push(mine, mine, lc_s.at[0], lc_r.at[core], sib)
    mine = rxr.at[core * NR + me_i]
    for dz in (4, 3, 5, 2, 6, 1, 7, 0):
        for dy in (1, 0):
            if (dy, dz) != (0, 0):
                for c in range(2):
                    push(mine, mine, lr_s.at[0], lr_r.at[core], (chip + c, at_cap(dy, dz)))
    push(mine, mine, lr_s.at[0], lr_r.at[core], sib)

    tb2[...] = jnp.zeros_like(tb2)
    for k, width in enumerate(WIDTH):
        sent(gi.at[pl.ds(0, 128), pl.ds(0, width)], first_s.at[k])

        @pl.when(core == k)
        def _():
            sent(gi.at[pl.ds(0, 384), pl.ds(0, width)], next_s.at[0])
            sent(gc.at[pl.ds(0, 320), pl.ds(0, width)], next_s.at[1])

        @pl.when(core != k)
        def _():
            for n in range(2):
                sent(gi.at[pl.ds(0, 16), pl.ds(0, width)], sib_s.at[n])

    arrived(sb.at[1 - core], ex_r.at[0])
    statistics(1 - core)

    arrived(rxc.at[pl.ds(0, NQ - 1)], lc_r.at[core])
    arrived(rxc.at[pl.ds(0, NQ)], lc_r.at[1 - core])
    arrived(rxr.at[pl.ds(0, NR - 1)], lr_r.at[core])
    arrived(rxr.at[pl.ds(0, NR)], lr_r.at[1 - core])
    tb2[0:1, :] = pool(rxr[0:NR])
    tb2[1:2, :] = pool(rxr[NR : 2 * NR])
    rows_all = tb2[...].T
    f_col_s = 0.5 * jnp.exp(cmx[0] - pool(rxc[0:NQ]))
    f_col_t = 0.25 * jnp.exp(cmx[1] - pool(rxc[NQ : 2 * NQ]))

    b = lax.broadcasted_iota(jnp.int32, (1, M), 1)
    t = jnp.where(b < MAIN, b >> 4, (b - MAIN) >> 2)
    u = jnp.where(b < MAIN, b & 15, 16 + (b & 3))
    col_id = cap * M + t * B + u
    for lo in range(0, M, 64):
        a = lo + lax.broadcasted_iota(jnp.int32, (64, 1), 0)
        t, u = (a >> 4, a & 15) if lo < MAIN else ((a - MAIN) >> 2, 16 + (a & 3))
        row_id = (at_img(0, 0) + (t & 1)) * (B * NR) + (t >> 1) * B + u
        here = slice(lo, lo + 64)
        f_row_s = 0.5 * jnp.exp(rmx[0, here, :] - rows_all[here, 0:1])
        f_row_t = 0.25 * jnp.exp(rmx[1, here, :] - rows_all[here, 1:2])
        g = er[0, here, :] * f_row_s + ec[0, here, :] * f_col_s
        g = g - (er[1, here, :] * f_row_t + ec[1, here, :] * f_col_t)
        g = g - jnp.where(row_id == col_id, 0.5, 0.0)
        tg[here, :] = g.astype(BF)

    def folded(v):
        v = jnp.concatenate([v[:, 256 * q : 256 * q + 256] for q in range(4)], axis=0)
        hi = v.astype(BF)
        lo = (v - hi.astype(F32)).astype(BF)
        return t_dot(fold, hi) + t_dot(fold, lo)

    def as_blocks():
        for h in range(2):
            here = slice(256 * h, 256 * h + 256)
            sg[here, 0:DS] = pg[here, :]
            sg[here, DS:W] = folded(pg[MAIN + 64 * h : MAIN + 64 * h + 64, :])

    def unfold(acc, out):
        out[0:16, :] = acc[:, 0:DS]
        for q in range(4):
            out[16:20, 256 * q : 256 * q + 256] = acc[4 * q : 4 * q + 4, DS:W]

    def finish():
        arrived(r_y, y_r.at[0])
        acc = own_c[...]
        for n in range(3):
            acc = acc + r_y[n].astype(F32)
        unfold(acc, oc_ref)
        arrived(r_z.at[pl.ds(0, NZ - 1)], z_r.at[0])
        r_z[z] = jnp.zeros((16, W), BF)
        acc = own_i[...]
        for n in range(NZ):
            acc = acc + r_z[n].astype(F32)
        unfold(acc, oi_ref)

    def drain():
        sent(sb.at[0], ex_s.at[0])
        sent(rxr.at[pl.ds(0, 2 * NR - 1)], lr_s.at[0])
        sent(rxc.at[pl.ds(0, 2 * NQ - 1)], lc_s.at[0])

    @pl.when(core == 0)
    def _():
        pg[...] = t_dot(tg[0:MAIN, :], gi[:, 256:W]) + t_dot(tg[MAIN:M, :], ar[...])
        as_blocks()
        order_y = (2, 1, 3, 0)
        for n, d in enumerate(order_y):
            s_x[n] = sg[rows((yh + d) % NYH, 32 * NX), :].astype(BF)
            for k, (dx, dev) in enumerate(((2, x2), (1, xu), (3, xd))):
                push(s_x.at[n, rows((x + dx) % NX, 32), :], r_x.at[3 * n + k], x_s.at[0], x_r.at[n], dev)
        drain()
        sent(gcs, ex_s.at[1])
        sent(brs, ex_s.at[2])
        for n, d in enumerate(order_y):
            v = sg[rows(slot_c(d, 0), 32), :]
            arrived(r_x.at[pl.ds(3 * n, 3)], x_r.at[n])
            for k in range(3):
                v = v + r_x[3 * n + k].astype(F32)
            if d:
                s_y[n] = v.astype(BF)
                for c in range(2):
                    push(s_y.at[n, pl.ds(16 * c, 16), :], r_y.at[n], y_s.at[0], y_r.at[0], (at_img(d, 0) + c, cap))
            else:
                own_c[...] = v[0:16, :]
                o_s[...] = v[16:32, :]
                push(o_s, own_c, o_send.at[0], o_r.at[0], sib)
        sent(r_x, x_s.at[0])
        arrived(own_i, o_r.at[0])
        finish()
        sent(s_y, y_s.at[0])
        sent(o_s, o_send.at[0])

    @pl.when(core == 1)
    def _():
        arrived(gcs, ex_r.at[1])
        arrived(brs, ex_r.at[2])
        pg[...] = dot(tg[:, 0:MAIN], gcs[...]) + dot(tg[:, MAIN:M], brs[...])
        as_blocks()
        for n in range(NZ):
            s_p[n] = sg[rows((1 - yl) * NZ + n, 32), :].astype(BF)
            push(s_p.at[n], r_p.at[n], p_s.at[0], p_r.at[n], pair)
        drain()
        for n in range(NZ):
            arrived(r_p.at[n], p_r.at[n])
            v = sg[rows(yl * NZ + n, 32), :] + r_p[n].astype(F32)
            s_z[n] = v.astype(BF)

            @pl.when(z != n)
            def _():
                for c in range(2):
                    push(s_z.at[n, pl.ds(16 * c, 16), :], r_z.at[z], z_s.at[0], z_r.at[0], (chip + c, yl * NZ + n))

            @pl.when(z == n)
            def _():
                own_i[...] = v[16:32, :]
                o_s[...] = v[0:16, :]
                push(o_s, own_i, o_send.at[0], o_r.at[0], sib)

        sent(s_p, p_s.at[0])
        arrived(own_c, o_r.at[0])
        finish()
        sent(s_z.at[pl.ds(0, NZ - 1)], z_s.at[0])
        sent(o_s, o_send.at[0])


def local(image_student, caption_student, image_teacher, caption_teacher):
    vmem = pl.BlockSpec(memory_space=pltpu.VMEM)
    dma = pltpu.SemaphoreType.DMA
    out = pltpu.VMEM((B, DS), F32)
    args = [
        pltpu.with_memory_space_constraint(a, pltpu.HBM)
        for a in (image_student, caption_student, image_teacher, caption_teacher)
    ]
    return pl.pallas_call(
        kernel,
        out_shape=(out, out),
        in_specs=[pl.BlockSpec(memory_space=pltpu.HBM)] * 4,
        out_specs=(vmem, vmem),
        scratch_shapes=[
            pltpu.VMEM((B, DS), BF),
            pltpu.VMEM((B, DS), BF),
            pltpu.VMEM((B, DT), BF),
            pltpu.VMEM((B, DT), BF),
            pltpu.VMEM((4, 16, 256), F32),
            pltpu.VMEM((2, 2, 16, W), BF),
            pltpu.VMEM((MAIN, W), BF),
            pltpu.VMEM((MAIN, W), BF),
            pltpu.VMEM((M - MAIN, DS), BF),
            pltpu.VMEM((M - MAIN, DS), BF),
            pltpu.VMEM((MAIN, DS), BF),
            pltpu.VMEM((M - MAIN, DS), BF),
            pltpu.VMEM((2, M, M), F32),
            pltpu.VMEM((2, M, M), F32),
            pltpu.VMEM((2, M, M), F32),
            pltpu.VMEM((2, M, 1), F32),
            pltpu.VMEM((2, 1, M), F32),
            pltpu.VMEM((M, 128), F32),
            pltpu.VMEM((128, M), F32),
            pltpu.VMEM((2 * NR, 1, M), F32),
            pltpu.VMEM((2 * NQ, 1, M), F32),
            pltpu.VMEM((M, M), BF),
            pltpu.VMEM((M, DS), F32),
            pltpu.VMEM((MAIN, W), F32),
            pltpu.VMEM((NZ, 32, W), BF),
            pltpu.VMEM((NZ, 32, W), BF),
            pltpu.VMEM((NZ, 32, W), BF),
            pltpu.VMEM((NZ, 16, W), BF),
            pltpu.VMEM((NYH, 32 * NX, W), BF),
            pltpu.VMEM((3 * NYH, 32, W), BF),
            pltpu.VMEM((3, 32, W), BF),
            pltpu.VMEM((3, 16, W), BF),
            pltpu.VMEM((16, W), F32),
            pltpu.VMEM((16, W), F32),
            pltpu.VMEM((16, W), F32),
            dma((4,)), dma((2,)), dma((2,)), dma((NR,)), dma((NQ,)), dma((2,)), dma((2,)),
            dma((3,)), dma((3,)), dma((2,)), dma((1,)), dma((2,)), dma((1,)),
            dma((NZ,)), dma((1,)), dma((1,)), dma((1,)),
            dma((NYH,)), dma((1,)), dma((1,)), dma((1,)), dma((1,)), dma((1,)),
        ],
        compiler_params=pltpu.CompilerParams(
            collective_id=0, has_side_effects=True, vmem_limit_bytes=56 * 2**20
        ),
        cost_estimate=pl.CostEstimate(flops=1_800_000_000, bytes_accessed=400_000, transcendentals=1_700_000),
        name="contrastive",
    )(*args)


def solution(mesh):
    return jax.shard_map(
        local,
        mesh=mesh,
        in_specs=(
            P(("img", "cap"), None),
            P(("cap", "img"), None),
            P(("img", "cap"), None),
            P(("cap", "img"), None),
        ),
        out_specs=(P(("img", "cap"), None), P(("cap", "img"), None)),
        check_vma=False,
    )
```

```python
import math

import jax
import jax.numpy as jnp
from jax import lax
from jax.experimental import pallas as pl
from jax.experimental.pallas import tpu as pltpu
from jax.sharding import PartitionSpec as P

MESH = pl.DeviceIdType.MESH
GAIN = 3.0
NX, NYH, NZ = 4, 4, 8
NR = NQ = 16
DS, DT = 1024, 768
W = 256 + DS
WIDTH = (256 + DS, 256 + DT)
B = 20
MAIN, M = 32 * NR, 40 * NR
BF, F32 = jnp.bfloat16, jnp.float32
ORDER = "P0U1D1L0R0Y1Y3E1F1U2D2X0L1R1Y2E2F2L3R3U3D3X1R2L2E3F3X3U4X2F4"


def dot_t(a, b):
    return lax.dot_general(a, b, (((1,), (1,)), ((), ())), preferred_element_type=F32)


def t_dot(a, b):
    return lax.dot_general(a, b, (((0,), (0,)), ((), ())), preferred_element_type=F32)


def dot(a, b):
    return jnp.dot(a, b, preferred_element_type=F32)


def fold_matrix():
    a = lax.broadcasted_iota(jnp.int32, (256, 256), 0)
    b = lax.broadcasted_iota(jnp.int32, (256, 256), 1)
    source = 16 * ((a >> 2) & 15) + 4 * (a >> 6) + (a & 3)
    return jnp.where(b == source, 1.0, 0.0).astype(BF)


def pool(parts):
    m = jnp.max(parts, axis=0)
    return m + jnp.log(jnp.sum(jnp.exp(parts - m[None]), axis=0))


def kernel(
    is_hbm, cs_hbm, it_hbm, ct_hbm, oi_ref, oc_ref,
    is_ref, cs_ref, it_ref, ct_ref, rp, pk, gi, gc, ar, br, gcs, brs,
    sb, er, ec, rmx, cmx, tb, tb2, rxr, rxc, tg,
    sg, s_p, r_p, s_z, r_z, s_x, r_x, s_y, r_y, own_i, own_c, o_s,
    in_sem, sib_r, sib_s, gi_r, gc_r, first_s, next_s, ex_r, ex_s, lr_r, lr_s, lc_r, lc_s,
    p_r, p_s, z_r, z_s, x_r, x_s, y_r, y_s, o_r, o_send,
):
    img, cap = lax.axis_index("img"), lax.axis_index("cap")
    yh, x, core = img // (2 * NX), (img // 2) % NX, img % 2
    yl, z = cap // NZ, cap % NZ

    def at_img(dyh, dx):
        return (((yh + dyh) % NYH) * NX + (x + dx) % NX) * 2

    def slot_c(dyh, dx):
        return ((yh + dyh) % NYH) * NX + (x + dx) % NX

    def at_cap(dyl, dz):
        return ((yl + dyl) % 2) * NZ + (z + dz) % NZ

    def rows(slot, n):
        return pl.ds(pl.multiple_of(n * slot, n), n)

    def remote(src, dst, send, recv, dev):
        return pltpu.make_async_remote_copy(
            src_ref=src, dst_ref=dst, send_sem=send, recv_sem=recv, device_id=dev, device_id_type=MESH
        )

    def push(src, dst, send, recv, dev):
        remote(src, dst, send, recv, dev).start()

    def sent(ref, sem):
        remote(ref, ref, sem, in_sem.at[0], sib).wait_send()

    up, down, pair = (img, at_cap(0, 1)), (img, at_cap(0, -1)), (img, at_cap(1, 0))
    xu, xd, x2 = [(at_img(0, d) + core, cap) for d in (1, -1, 2)]
    ys = [(at_img(d, 0) + core, cap) for d in (1, 2, 3)]
    sib = (at_img(0, 0) + 1 - core, cap)

    def arrived(ref, sem):
        remote(ref, ref, in_sem.at[0], sem, sib).wait_recv()

    barrier = pltpu.get_barrier_semaphore()
    chip = at_img(0, 0)
    around_i = [(chip, at_cap(1, 0)), (chip, at_cap(0, 1)), (chip, at_cap(0, -1))]
    around_c = [(at_img(*d), cap) for d in ((2, 0), (1, 0), (3, 0), (0, 1), (0, -1))]
    near = [sib] + [(dev[0] + c, dev[1]) for dev in around_i + around_c for c in range(2)]
    for dev in near:
        pl.semaphore_signal(barrier, inc=1, device_id=dev, device_id_type=MESH)

    loads = []
    for n, (src, dst) in enumerate(((is_hbm, is_ref), (it_hbm, it_ref), (cs_hbm, cs_ref), (ct_hbm, ct_ref))):
        c = pltpu.make_async_copy(src, dst, in_sem.at[n])
        c.start()
        loads.append(c)
    for c in loads:
        c.wait()

    for n, (k, j, src, width) in enumerate(
        ((0, 0, is_ref, DS), (1, 0, it_ref, DT), (0, 1, cs_ref, DS), (1, 1, ct_ref, DT))
    ):
        pk[k, j, :, 256 : 256 + width] = src[0:16, :]
        if width < DS:
            pk[k, j, :, 256 + width : W] = jnp.zeros((16, DS - width), BF)
        last = src[...].astype(F32)[16:20, :]
        rp[n] = jnp.zeros((16, 256), F32)
        for q in range(width // 256):
            rp[n, 4 * q : 4 * q + 4, :] = last[:, 256 * q : 256 * q + 256]
        pk[k, j, :, 0:256] = rp[n].astype(BF)

    @pl.when(core == 1)
    def _():
        gi[:, 256 + DT : W] = jnp.zeros((MAIN, DS - DT), BF)
        gc[:, 256 + DT : W] = jnp.zeros((MAIN, DS - DT), BF)

    pl.semaphore_wait(barrier, len(near))

    me_i, me_c = cap, slot_c(0, 0)
    mine_i, mine_c = rows(2 * me_i + core, 16), rows(2 * me_c + core, 16)
    for k, width in enumerate(WIDTH):

        @pl.when(core != k)
        def _():
            w = pl.ds(0, width)
            push(pk.at[k, 0, :, w], gi.at[mine_i, w], sib_s.at[0], sib_r.at[0], sib)
            push(pk.at[k, 1, :, w], gc.at[mine_c, w], sib_s.at[1], sib_r.at[1], sib)

    for dev in around_i:
        for k, width in enumerate(WIDTH):
            w = pl.ds(0, width)
            push(pk.at[k, 0, :, w], gi.at[mine_i, w], first_s.at[k], gi_r.at[me_i], (dev[0] + k, dev[1]))

    def own_caption(dev):
        for k, width in enumerate(WIDTH):
            w = pl.ds(0, width)
            push(pk.at[k, 1, :, w], gc.at[mine_c, w], first_s.at[k], gc_r.at[me_c], (dev[0] + k, dev[1]))

    for dev in around_c[3:] + around_c[1:3]:
        own_caption(dev)
    gi[mine_i, :] = pk[core, 0]
    gc[mine_c, :] = pk[core, 1]

    flow = {}
    for k in (1, 2, 3):
        flow["U%d" % k] = (at_cap(0, -k), (up,))
        flow["D%d" % k] = (at_cap(0, k), (down,) if k < 3 else ())
        flow["E%d" % k] = (at_cap(1, -k), (up,) if k < 3 else ())
        flow["F%d" % k] = (at_cap(1, k), (down,))
    flow["P0"] = (at_cap(1, 0), (up, down))
    flow["U4"] = (at_cap(0, -4), ())
    flow["F4"] = (at_cap(1, 4), ())
    for j in range(NYH):
        if j:
            flow["Y%d" % j] = (slot_c(j, 0), (xu, xd))
        flow["L%d" % j] = (slot_c(j, -1), (xu,) if j < 2 else ())
        flow["R%d" % j] = (slot_c(j, 1), (xd,) if j >= 2 else ())
        flow["X%d" % j] = (slot_c(j, 2), ())

    def caption(slot):
        push(gc.at[rows(slot, 32), pl.ds(256, DS)], gcs.at[rows(slot, 32), :], ex_s.at[1], ex_r.at[1], sib)

    for k, width in enumerate(WIDTH):

        @pl.when(core == k)
        def _():
            for n in range(0, len(ORDER), 2):
                name = ORDER[n : n + 2]
                if n == 6:
                    own_caption(around_c[0])
                    arrived(gi.at[rows(2 * me_i + 1 - core, 16), pl.ds(0, width)], sib_r.at[0])
                    arrived(gc.at[rows(2 * me_c + 1 - core, 16), pl.ds(0, width)], sib_r.at[1])
                slot, devs = flow[name]
                buf, recv, send = (gc, gc_r, next_s.at[1]) if name[0] in "YLRX" else (gi, gi_r, next_s.at[0])
                block = buf.at[rows(slot, 32), pl.ds(0, width)]
                arrived(block, recv.at[slot])
                for dev in devs:
                    push(block, block, send, recv.at[slot], dev)
                if k == 0 and n == len(ORDER) - 12:
                    for j in range(NYH):
                        for d in (0, 1, 3) if j > 1 else range(NX):
                            caption(slot_c(j, d))
                if k == 0 and name[0] == "X" and n > len(ORDER) - 12:
                    caption(slot)

    fold = fold_matrix()
    for src, dst in ((gi, ar), (gc, br)):
        for h in range(2):
            y = dot(fold, src[256 * h : 256 * h + 256, 0:256]).astype(BF)
            for q in range(4):
                dst[64 * h : 64 * h + 64, 256 * q : 256 * q + 256] = y[64 * q : 64 * q + 64, :]

    @pl.when(core == 0)
    def _():
        push(br, brs, ex_s.at[2], ex_r.at[2], sib)

    gain = jnp.where(core == 0, GAIN / math.sqrt(DS), GAIN / math.sqrt(DT))
    sb[core, 0:MAIN, 0:MAIN] = gain * dot_t(gi[:, 256:W], gc[:, 256:W])
    sb[core, 0:MAIN, MAIN:M] = gain * dot_t(gi[:, 256:W], br[...])
    sb[core, MAIN:M, 0:MAIN] = gain * dot_t(ar[...], gc[:, 256:W])
    sb[core, MAIN:M, MAIN:M] = gain * dot_t(ar[...], br[...])
    push(sb.at[core], sb.at[core], ex_s.at[0], ex_r.at[0], sib)

    def statistics(k):
        top, total, lses = None, None, []
        for b in range(0, M, 64):
            blk = sb[k, b : b + 64, :]
            m = jnp.max(blk, axis=1, keepdims=True)
            rmx[k, b : b + 64, :] = m
            e = jnp.exp(blk - m)
            er[k, b : b + 64, :] = e
            lses.append(m + jnp.log(jnp.sum(e, axis=1, keepdims=True)))
            t = jnp.max(blk, axis=0, keepdims=True)
            top = t if top is None else jnp.maximum(top, t)
        for b in range(0, M, 64):
            e = jnp.exp(sb[k, b : b + 64, :] - top)
            ec[k, b : b + 64, :] = e
            t = jnp.sum(e, axis=0, keepdims=True)
            total = t if total is None else total + t
        cmx[k] = top
        return lses, top + jnp.log(total)

    row_lse, col_lse = statistics(core)

    rxc[core * NQ + me_c] = col_lse
    for n, b in enumerate(range(0, M, 64)):
        tb[b : b + 64, :] = jnp.broadcast_to(row_lse[n], (64, 128))
    rxr[core * NR + me_i] = tb[...].T[0:1, :]
    mine_c, mine_r = rxc.at[core * NQ + me_c], rxr.at[core * NR + me_i]
    far = [(2 * min(j, 4 - j) + min(d, 4 - d), j, d, True) for j in range(NYH) for d in range(NX)]
    far += [(j + min(d, 8 - d), j, d, False) for j in range(2) for d in range(NZ)]
    for hops, j, d, of_columns in sorted(far, reverse=True):
        if hops:
            for c in range(2):
                if of_columns:
                    push(mine_c, mine_c, lc_s.at[0], lc_r.at[core], (at_img(j, d) + c, cap))
                else:
                    push(mine_r, mine_r, lr_s.at[0], lr_r.at[core], (chip + c, at_cap(j, d)))
    push(mine_c, mine_c, lc_s.at[0], lc_r.at[core], sib)
    push(mine_r, mine_r, lr_s.at[0], lr_r.at[core], sib)

    tb2[...] = jnp.zeros_like(tb2)
    for k, width in enumerate(WIDTH):
        sent(gi.at[pl.ds(0, 128), pl.ds(0, width)], first_s.at[k])

        @pl.when(core == k)
        def _():
            sent(gi.at[pl.ds(0, 384), pl.ds(0, width)], next_s.at[0])
            sent(gc.at[pl.ds(0, 320), pl.ds(0, width)], next_s.at[1])

        @pl.when(core != k)
        def _():
            for n in range(2):
                sent(gi.at[pl.ds(0, 16), pl.ds(0, width)], sib_s.at[n])

    arrived(sb.at[1 - core], ex_r.at[0])
    statistics(1 - core)

    arrived(rxc.at[pl.ds(0, NQ - 1)], lc_r.at[core])
    arrived(rxc.at[pl.ds(0, NQ)], lc_r.at[1 - core])
    arrived(rxr.at[pl.ds(0, NR - 1)], lr_r.at[core])
    arrived(rxr.at[pl.ds(0, NR)], lr_r.at[1 - core])
    tb2[0:1, :] = pool(rxr[0:NR])
    tb2[1:2, :] = pool(rxr[NR : 2 * NR])
    rows_all = tb2[...].T
    f_col_s = 0.5 * jnp.exp(cmx[0] - pool(rxc[0:NQ]))
    f_col_t = 0.25 * jnp.exp(cmx[1] - pool(rxc[NQ : 2 * NQ]))

    b = lax.broadcasted_iota(jnp.int32, (1, M), 1)
    t = jnp.where(b < MAIN, b >> 4, (b - MAIN) >> 2)
    u = jnp.where(b < MAIN, b & 15, 16 + (b & 3))
    col_id = cap * M + t * B + u
    for lo in range(0, M, 64):
        a = lo + lax.broadcasted_iota(jnp.int32, (64, 1), 0)
        t, u = (a >> 4, a & 15) if lo < MAIN else ((a - MAIN) >> 2, 16 + (a & 3))
        row_id = (at_img(0, 0) + (t & 1)) * (B * NR) + (t >> 1) * B + u
        here = slice(lo, lo + 64)
        f_row_s = 0.5 * jnp.exp(rmx[0, here, :] - rows_all[here, 0:1])
        f_row_t = 0.25 * jnp.exp(rmx[1, here, :] - rows_all[here, 1:2])
        g = er[0, here, :] * f_row_s + ec[0, here, :] * f_col_s
        g = g - (er[1, here, :] * f_row_t + ec[1, here, :] * f_col_t)
        g = g - jnp.where(row_id == col_id, 0.5, 0.0)
        tg[here, :] = g.astype(BF)

    def folded(v):
        v = jnp.concatenate([v[:, 256 * q : 256 * q + 256] for q in range(4)], axis=0)
        hi = v.astype(BF)
        lo = (v - hi.astype(F32)).astype(BF)
        return t_dot(fold, hi) + t_dot(fold, lo)

    def unfold(acc, out):
        out[0:16, :] = acc[:, 0:DS]
        for q in range(4):
            out[16:20, 256 * q : 256 * q + 256] = acc[4 * q : 4 * q + 4, DS:W]

    def finish():
        arrived(r_y, y_r.at[0])
        acc = own_c[...]
        for n in range(3):
            acc = acc + r_y[n].astype(F32)
        unfold(acc, oc_ref)
        arrived(r_z.at[pl.ds(0, NZ - 1)], z_r.at[0])
        r_z[z] = jnp.zeros((16, W), BF)
        acc = own_i[...]
        for n in range(NZ):
            acc = acc + r_z[n].astype(F32)
        unfold(acc, oi_ref)

    def drain():
        sent(sb.at[0], ex_s.at[0])
        sent(rxr.at[pl.ds(0, 2 * NR - 1)], lr_s.at[0])
        sent(rxc.at[pl.ds(0, 2 * NQ - 1)], lc_s.at[0])

    @pl.when(core == 0)
    def _():
        last = t_dot(tg[0:MAIN, MAIN:M], gi[:, 256:W]) + t_dot(tg[MAIN:M, MAIN:M], ar[...])
        for h in range(2):
            sg[256 * h : 256 * h + 256, DS:W] = folded(last[64 * h : 64 * h + 64, :])
        order_y = (2, 1, 3, 0)
        for n, d in enumerate(order_y):
            group = rows((yh + d) % NYH, 32 * NX)
            sg[group, 0:DS] = t_dot(tg[0:MAIN, group], gi[:, 256:W]) + t_dot(tg[MAIN:M, group], ar[...])
            s_x[n] = sg[group, :].astype(BF)
            for k, (dx, dev) in enumerate(((2, x2), (1, xu), (3, xd))):
                push(s_x.at[n, rows((x + dx) % NX, 32), :], r_x.at[3 * n + k], x_s.at[0], x_r.at[n], dev)
        drain()
        sent(gcs, ex_s.at[1])
        sent(brs, ex_s.at[2])
        for n, d in enumerate(order_y):
            v = sg[rows(slot_c(d, 0), 32), :]
            arrived(r_x.at[pl.ds(3 * n, 3)], x_r.at[n])
            for k in range(3):
                v = v + r_x[3 * n + k].astype(F32)
            if d:
                s_y[n] = v.astype(BF)
                for c in range(2):
                    push(s_y.at[n, pl.ds(16 * c, 16), :], r_y.at[n], y_s.at[0], y_r.at[0], (at_img(d, 0) + c, cap))
            else:
                own_c[...] = v[0:16, :]
                o_s[...] = v[16:32, :]
                push(o_s, own_c, o_send.at[0], o_r.at[0], sib)
        sent(r_x, x_s.at[0])
        arrived(own_i, o_r.at[0])
        finish()
        sent(s_y, y_s.at[0])
        sent(o_s, o_send.at[0])

    @pl.when(core == 1)
    def _():
        arrived(gcs, ex_r.at[1])
        arrived(brs, ex_r.at[2])
        last = dot(tg[MAIN:M, 0:MAIN], gcs[...]) + dot(tg[MAIN:M, MAIN:M], brs[...])
        for h in range(2):
            sg[256 * h : 256 * h + 256, DS:W] = folded(last[64 * h : 64 * h + 64, :])
        for m in range(4):
            group = rows(2 * ((1 - yl) if m < 2 else yl) + m % 2, 128)
            sg[group, 0:DS] = dot(tg[group, 0:MAIN], gcs[...]) + dot(tg[group, MAIN:M], brs[...])
            if m < 2:
                for n in range(4 * m, 4 * m + 4):
                    s_p[n] = sg[rows((1 - yl) * NZ + n, 32), :].astype(BF)
                    push(s_p.at[n], r_p.at[n], p_s.at[0], p_r.at[n], pair)
        drain()
        for n in range(NZ):
            arrived(r_p.at[n], p_r.at[n])
            v = sg[rows(yl * NZ + n, 32), :] + r_p[n].astype(F32)
            s_z[n] = v.astype(BF)

            @pl.when(z != n)
            def _():
                for c in range(2):
                    push(s_z.at[n, pl.ds(16 * c, 16), :], r_z.at[z], z_s.at[0], z_r.at[0], (chip + c, yl * NZ + n))

            @pl.when(z == n)
            def _():
                own_i[...] = v[16:32, :]
                o_s[...] = v[0:16, :]
                push(o_s, own_i, o_send.at[0], o_r.at[0], sib)

        sent(s_p, p_s.at[0])
        arrived(own_c, o_r.at[0])
        finish()
        sent(s_z.at[pl.ds(0, NZ - 1)], z_s.at[0])
        sent(o_s, o_send.at[0])


def local(image_student, caption_student, image_teacher, caption_teacher):
    vmem = pl.BlockSpec(memory_space=pltpu.VMEM)
    dma = pltpu.SemaphoreType.DMA
    out = pltpu.VMEM((B, DS), F32)
    args = [
        pltpu.with_memory_space_constraint(a, pltpu.HBM)
        for a in (image_student, caption_student, image_teacher, caption_teacher)
    ]
    return pl.pallas_call(
        kernel,
        out_shape=(out, out),
        in_specs=[pl.BlockSpec(memory_space=pltpu.HBM)] * 4,
        out_specs=(vmem, vmem),
        scratch_shapes=[
            pltpu.VMEM((B, DS), BF),
            pltpu.VMEM((B, DS), BF),
            pltpu.VMEM((B, DT), BF),
            pltpu.VMEM((B, DT), BF),
            pltpu.VMEM((4, 16, 256), F32),
            pltpu.VMEM((2, 2, 16, W), BF),
            pltpu.VMEM((MAIN, W), BF),
            pltpu.VMEM((MAIN, W), BF),
            pltpu.VMEM((M - MAIN, DS), BF),
            pltpu.VMEM((M - MAIN, DS), BF),
            pltpu.VMEM((MAIN, DS), BF),
            pltpu.VMEM((M - MAIN, DS), BF),
            pltpu.VMEM((2, M, M), F32),
            pltpu.VMEM((2, M, M), F32),
            pltpu.VMEM((2, M, M), F32),
            pltpu.VMEM((2, M, 1), F32),
            pltpu.VMEM((2, 1, M), F32),
            pltpu.VMEM((M, 128), F32),
            pltpu.VMEM((128, M), F32),
            pltpu.VMEM((2 * NR, 1, M), F32),
            pltpu.VMEM((2 * NQ, 1, M), F32),
            pltpu.VMEM((M, M), BF),
            pltpu.VMEM((MAIN, W), F32),
            pltpu.VMEM((NZ, 32, W), BF),
            pltpu.VMEM((NZ, 32, W), BF),
            pltpu.VMEM((NZ, 32, W), BF),
            pltpu.VMEM((NZ, 16, W), BF),
            pltpu.VMEM((NYH, 32 * NX, W), BF),
            pltpu.VMEM((3 * NYH, 32, W), BF),
            pltpu.VMEM((3, 32, W), BF),
            pltpu.VMEM((3, 16, W), BF),
            pltpu.VMEM((16, W), F32),
            pltpu.VMEM((16, W), F32),
            pltpu.VMEM((16, W), F32),
            dma((4,)), dma((2,)), dma((2,)), dma((NR,)), dma((NQ,)), dma((2,)), dma((2,)),
            dma((3,)), dma((3,)), dma((2,)), dma((1,)), dma((2,)), dma((1,)),
            dma((NZ,)), dma((1,)), dma((1,)), dma((1,)),
            dma((NYH,)), dma((1,)), dma((1,)), dma((1,)), dma((1,)), dma((1,)),
        ],
        compiler_params=pltpu.CompilerParams(
            collective_id=0, has_side_effects=True, vmem_limit_bytes=56 * 2**20
        ),
        cost_estimate=pl.CostEstimate(flops=1_800_000_000, bytes_accessed=400_000, transcendentals=1_700_000),
        name="contrastive",
    )(*args)


def solution(mesh):
    return jax.shard_map(
        local,
        mesh=mesh,
        in_specs=(
            P(("img", "cap"), None),
            P(("cap", "img"), None),
            P(("img", "cap"), None),
            P(("cap", "img"), None),
        ),
        out_specs=(P(("img", "cap"), None), P(("cap", "img"), None)),
        check_vma=False,
    )
```

```python
import math

import jax
import jax.numpy as jnp
from jax import lax
from jax.experimental import pallas as pl
from jax.experimental.pallas import tpu as pltpu
from jax.sharding import PartitionSpec as P

MESH = pl.DeviceIdType.MESH
GAIN = 3.0
NX, NYH, NZ = 4, 4, 8
NR = NQ = 16
DS, DT = 1024, 768
W = 256 + DS
WIDTH = (256 + DS, 256 + DT)
B = 20
MAIN, M = 32 * NR, 40 * NR
BF, F32 = jnp.bfloat16, jnp.float32
FAR_Z = (4, 3, 5, 2, 6, 1, 7, 0)
ORDER = "P0U1D1L0R0Y1Y3E1F1U2D2X0L1R1Y2E2F2L3R3U3D3X1R2L2E3F3X3U4X2F4"


def dot_t(a, b):
    return lax.dot_general(a, b, (((1,), (1,)), ((), ())), preferred_element_type=F32)


def t_dot(a, b):
    return lax.dot_general(a, b, (((0,), (0,)), ((), ())), preferred_element_type=F32)


def dot(a, b):
    return jnp.dot(a, b, preferred_element_type=F32)


def fold_matrix():
    a = lax.broadcasted_iota(jnp.int32, (256, 256), 0)
    b = lax.broadcasted_iota(jnp.int32, (256, 256), 1)
    source = 16 * ((a >> 2) & 15) + 4 * (a >> 6) + (a & 3)
    return jnp.where(b == source, 1.0, 0.0).astype(BF)


def pool(parts):
    m = jnp.max(parts, axis=0)
    return m + jnp.log(jnp.sum(jnp.exp(parts - m[None]), axis=0))


def kernel(
    is_hbm, cs_hbm, it_hbm, ct_hbm, oi_ref, oc_ref,
    is_ref, cs_ref, it_ref, ct_ref, rp, pk, gi, gc, ar, br, gcs, brs,
    sb, er, ec, rmx, cmx, tb, tb2, rxr, rxc, tg,
    sg, s_p, r_p, s_z, r_z, s_x, r_x, s_y, r_y, own_i, own_c, o_s,
    in_sem, sib_r, sib_s, gi_r, gc_r, first_s, next_s, ex_r, ex_s, lr_r, lr_s, lc_r, lc_s,
    p_r, p_s, z_r, z_s, x_r, x_s, y_r, y_s, o_r, o_send,
):
    img, cap = lax.axis_index("img"), lax.axis_index("cap")
    yh, x, core = img // (2 * NX), (img // 2) % NX, img % 2
    yl, z = cap // NZ, cap % NZ

    def at_img(dyh, dx):
        return (((yh + dyh) % NYH) * NX + (x + dx) % NX) * 2

    def slot_c(dyh, dx):
        return ((yh + dyh) % NYH) * NX + (x + dx) % NX

    def at_cap(dyl, dz):
        return ((yl + dyl) % 2) * NZ + (z + dz) % NZ

    def rows(slot, n):
        return pl.ds(pl.multiple_of(n * slot, n), n)

    def remote(src, dst, send, recv, dev):
        return pltpu.make_async_remote_copy(
            src_ref=src, dst_ref=dst, send_sem=send, recv_sem=recv, device_id=dev, device_id_type=MESH
        )

    def push(src, dst, send, recv, dev):
        remote(src, dst, send, recv, dev).start()

    def sent(ref, sem):
        remote(ref, ref, sem, in_sem.at[0], sib).wait_send()

    up, down, pair = (img, at_cap(0, 1)), (img, at_cap(0, -1)), (img, at_cap(1, 0))
    xu, xd, x2 = [(at_img(0, d) + core, cap) for d in (1, -1, 2)]
    ys = [(at_img(d, 0) + core, cap) for d in (1, 2, 3)]
    sib = (at_img(0, 0) + 1 - core, cap)

    def arrived(ref, sem):
        remote(ref, ref, in_sem.at[0], sem, sib).wait_recv()

    barrier = pltpu.get_barrier_semaphore()
    chip = at_img(0, 0)
    around_i = [(chip, at_cap(1, 0)), (chip, at_cap(0, 1)), (chip, at_cap(0, -1))]
    around_c = [(at_img(*d), cap) for d in ((2, 0), (1, 0), (3, 0), (0, 1), (0, -1))]
    near = [sib] + [(dev[0] + c, dev[1]) for dev in around_i + around_c for c in range(2)]
    for dev in near:
        pl.semaphore_signal(barrier, inc=1, device_id=dev, device_id_type=MESH)

    loads = []
    for n, (src, dst) in enumerate(((is_hbm, is_ref), (it_hbm, it_ref), (cs_hbm, cs_ref), (ct_hbm, ct_ref))):
        c = pltpu.make_async_copy(src, dst, in_sem.at[n])
        c.start()
        loads.append(c)
    for c in loads:
        c.wait()

    for n, (k, j, src, width) in enumerate(
        ((0, 0, is_ref, DS), (1, 0, it_ref, DT), (0, 1, cs_ref, DS), (1, 1, ct_ref, DT))
    ):
        pk[k, j, :, 256 : 256 + width] = src[0:16, :]
        if width < DS:
            pk[k, j, :, 256 + width : W] = jnp.zeros((16, DS - width), BF)
        last = src[...].astype(F32)[16:20, :]
        rp[n] = jnp.zeros((16, 256), F32)
        for q in range(width // 256):
            rp[n, 4 * q : 4 * q + 4, :] = last[:, 256 * q : 256 * q + 256]
        pk[k, j, :, 0:256] = rp[n].astype(BF)

    @pl.when(core == 1)
    def _():
        gi[:, 256 + DT : W] = jnp.zeros((MAIN, DS - DT), BF)
        gc[:, 256 + DT : W] = jnp.zeros((MAIN, DS - DT), BF)

    pl.semaphore_wait(barrier, len(near))

    me_i, me_c = cap, slot_c(0, 0)
    mine_i, mine_c = rows(2 * me_i + core, 16), rows(2 * me_c + core, 16)
    for k, width in enumerate(WIDTH):

        @pl.when(core != k)
        def _():
            w = pl.ds(0, width)
            push(pk.at[k, 0, :, w], gi.at[mine_i, w], sib_s.at[0], sib_r.at[0], sib)
            push(pk.at[k, 1, :, w], gc.at[mine_c, w], sib_s.at[1], sib_r.at[1], sib)

    for dev in around_i:
        for k, width in enumerate(WIDTH):
            w = pl.ds(0, width)
            push(pk.at[k, 0, :, w], gi.at[mine_i, w], first_s.at[k], gi_r.at[me_i], (dev[0] + k, dev[1]))

    def own_caption(dev):
        for k, width in enumerate(WIDTH):
            w = pl.ds(0, width)
            push(pk.at[k, 1, :, w], gc.at[mine_c, w], first_s.at[k], gc_r.at[me_c], (dev[0] + k, dev[1]))

    for dev in around_c[3:] + around_c[1:3]:
        own_caption(dev)
    gi[mine_i, :] = pk[core, 0]
    gc[mine_c, :] = pk[core, 1]

    flow = {}
    for k in (1, 2, 3):
        flow["U%d" % k] = (at_cap(0, -k), (up,))
        flow["D%d" % k] = (at_cap(0, k), (down,) if k < 3 else ())
        flow["E%d" % k] = (at_cap(1, -k), (up,) if k < 3 else ())
        flow["F%d" % k] = (at_cap(1, k), (down,))
    flow["P0"] = (at_cap(1, 0), (up, down))
    flow["U4"] = (at_cap(0, -4), ())
    flow["F4"] = (at_cap(1, 4), ())
    for j in range(NYH):
        if j:
            flow["Y%d" % j] = (slot_c(j, 0), (xu, xd))
        flow["L%d" % j] = (slot_c(j, -1), (xu,) if j < 2 else ())
        flow["R%d" % j] = (slot_c(j, 1), (xd,) if j >= 2 else ())
        flow["X%d" % j] = (slot_c(j, 2), ())

    def caption(slot):
        push(gc.at[rows(slot, 32), pl.ds(256, DS)], gcs.at[rows(slot, 32), :], ex_s.at[1], ex_r.at[1], sib)

    for k, width in enumerate(WIDTH):

        @pl.when(core == k)
        def _():
            for n in range(0, len(ORDER), 2):
                name = ORDER[n : n + 2]
                if n == 6:
                    own_caption(around_c[0])
                    arrived(gi.at[rows(2 * me_i + 1 - core, 16), pl.ds(0, width)], sib_r.at[0])
                    arrived(gc.at[rows(2 * me_c + 1 - core, 16), pl.ds(0, width)], sib_r.at[1])
                slot, devs = flow[name]
                buf, recv, send = (gc, gc_r, next_s.at[1]) if name[0] in "YLRX" else (gi, gi_r, next_s.at[0])
                block = buf.at[rows(slot, 32), pl.ds(0, width)]
                arrived(block, recv.at[slot])
                for dev in devs:
                    push(block, block, send, recv.at[slot], dev)
                if k == 0 and n == len(ORDER) - 12:
                    for j in range(NYH):
                        for d in (0, 1, 3) if j > 1 else range(NX):
                            caption(slot_c(j, d))
                if k == 0 and name[0] == "X" and n > len(ORDER) - 12:
                    caption(slot)

    fold = fold_matrix()
    for src, dst in ((gi, ar), (gc, br)):
        for h in range(2):
            y = dot(fold, src[256 * h : 256 * h + 256, 0:256]).astype(BF)
            for q in range(4):
                dst[64 * h : 64 * h + 64, 256 * q : 256 * q + 256] = y[64 * q : 64 * q + 64, :]

    @pl.when(core == 0)
    def _():
        push(br, brs, ex_s.at[2], ex_r.at[2], sib)

    gain = jnp.where(core == 0, GAIN / math.sqrt(DS), GAIN / math.sqrt(DT))
    sb[core, 0:MAIN, 0:MAIN] = gain * dot_t(gi[:, 256:W], gc[:, 256:W])
    sb[core, 0:MAIN, MAIN:M] = gain * dot_t(gi[:, 256:W], br[...])
    sb[core, MAIN:M, 0:MAIN] = gain * dot_t(ar[...], gc[:, 256:W])
    sb[core, MAIN:M, MAIN:M] = gain * dot_t(ar[...], br[...])
    push(sb.at[core], sb.at[core], ex_s.at[0], ex_r.at[0], sib)

    def statistics(k):
        top, total, lses = None, None, []
        for b in range(0, M, 64):
            blk = sb[k, b : b + 64, :]
            m = jnp.max(blk, axis=1, keepdims=True)
            rmx[k, b : b + 64, :] = m
            e = jnp.exp(blk - m)
            er[k, b : b + 64, :] = e
            lses.append(m + jnp.log(jnp.sum(e, axis=1, keepdims=True)))
            t = jnp.max(blk, axis=0, keepdims=True)
            top = t if top is None else jnp.maximum(top, t)
        for b in range(0, M, 64):
            e = jnp.exp(sb[k, b : b + 64, :] - top)
            ec[k, b : b + 64, :] = e
            t = jnp.sum(e, axis=0, keepdims=True)
            total = t if total is None else total + t
        cmx[k] = top
        return lses, top + jnp.log(total)

    row_lse, col_lse = statistics(core)

    rxc[core * NQ + me_c] = col_lse
    for n, b in enumerate(range(0, M, 64)):
        tb[b : b + 64, :] = jnp.broadcast_to(row_lse[n], (64, 128))
    rxr[core * NR + me_i] = tb[...].T[0:1, :]
    mine_c, mine_r = rxc.at[core * NQ + me_c], rxr.at[core * NR + me_i]
    far = [(2 * min(j, 4 - j) + min(d, 4 - d), j, d, True) for j in range(NYH) for d in range(NX)]
    far += [(j + min(d, 8 - d), j, d, False) for j in range(2) for d in range(NZ)]
    for hops, j, d, of_columns in sorted(far, reverse=True):
        if hops:
            for c in range(2):
                if of_columns:
                    push(mine_c, mine_c, lc_s.at[0], lc_r.at[core], (at_img(j, d) + c, cap))
                else:
                    push(mine_r, mine_r, lr_s.at[0], lr_r.at[core], (chip + c, at_cap(j, d)))
    push(mine_c, mine_c, lc_s.at[0], lc_r.at[core], sib)
    push(mine_r, mine_r, lr_s.at[0], lr_r.at[core], sib)

    tb2[...] = jnp.zeros_like(tb2)
    for k, width in enumerate(WIDTH):
        sent(gi.at[pl.ds(0, 128), pl.ds(0, width)], first_s.at[k])

        @pl.when(core == k)
        def _():
            sent(gi.at[pl.ds(0, 384), pl.ds(0, width)], next_s.at[0])
            sent(gc.at[pl.ds(0, 320), pl.ds(0, width)], next_s.at[1])

        @pl.when(core != k)
        def _():
            for n in range(2):
                sent(gi.at[pl.ds(0, 16), pl.ds(0, width)], sib_s.at[n])

    arrived(sb.at[1 - core], ex_r.at[0])
    statistics(1 - core)

    arrived(rxc.at[pl.ds(0, NQ - 1)], lc_r.at[core])
    arrived(rxc.at[pl.ds(0, NQ)], lc_r.at[1 - core])
    arrived(rxr.at[pl.ds(0, NR - 1)], lr_r.at[core])
    arrived(rxr.at[pl.ds(0, NR)], lr_r.at[1 - core])
    tb2[0:1, :] = pool(rxr[0:NR])
    tb2[1:2, :] = pool(rxr[NR : 2 * NR])
    rows_all = tb2[...].T
    f_col_s = 0.5 * jnp.exp(cmx[0] - pool(rxc[0:NQ]))
    f_col_t = 0.25 * jnp.exp(cmx[1] - pool(rxc[NQ : 2 * NQ]))

    b = lax.broadcasted_iota(jnp.int32, (1, M), 1)
    t = jnp.where(b < MAIN, b >> 4, (b - MAIN) >> 2)
    u = jnp.where(b < MAIN, b & 15, 16 + (b & 3))
    col_id = cap * M + t * B + u
    for lo in range(0, M, 64):
        a = lo + lax.broadcasted_iota(jnp.int32, (64, 1), 0)
        t, u = (a >> 4, a & 15) if lo < MAIN else ((a - MAIN) >> 2, 16 + (a & 3))
        row_id = (at_img(0, 0) + (t & 1)) * (B * NR) + (t >> 1) * B + u
        here = slice(lo, lo + 64)
        f_row_s = 0.5 * jnp.exp(rmx[0, here, :] - rows_all[here, 0:1])
        f_row_t = 0.25 * jnp.exp(rmx[1, here, :] - rows_all[here, 1:2])
        g = er[0, here, :] * f_row_s + ec[0, here, :] * f_col_s
        g = g - (er[1, here, :] * f_row_t + ec[1, here, :] * f_col_t)
        g = g - jnp.where(row_id == col_id, 0.5, 0.0)
        tg[here, :] = g.astype(BF)

    def folded(v):
        v = jnp.concatenate([v[:, 256 * q : 256 * q + 256] for q in range(4)], axis=0)
        hi = v.astype(BF)
        lo = (v - hi.astype(F32)).astype(BF)
        return t_dot(fold, hi) + t_dot(fold, lo)

    def unfold(acc, out):
        out[0:16, :] = acc[:, 0:DS]
        for q in range(4):
            out[16:20, 256 * q : 256 * q + 256] = acc[4 * q : 4 * q + 4, DS:W]

    def finish():
        arrived(r_y, y_r.at[0])
        acc = own_c[...]
        for n in range(3):
            acc = acc + r_y[n].astype(F32)
        unfold(acc, oc_ref)
        arrived(r_z.at[pl.ds(0, NZ - 1)], z_r.at[0])
        r_z[z] = jnp.zeros((16, W), BF)
        acc = own_i[...]
        for n in range(NZ):
            acc = acc + r_z[n].astype(F32)
        unfold(acc, oi_ref)

    def drain():
        sent(sb.at[0], ex_s.at[0])
        sent(rxr.at[pl.ds(0, 2 * NR - 1)], lr_s.at[0])
        sent(rxc.at[pl.ds(0, 2 * NQ - 1)], lc_s.at[0])

    @pl.when(core == 0)
    def _():
        last = t_dot(tg[0:MAIN, MAIN:M], gi[:, 256:W]) + t_dot(tg[MAIN:M, MAIN:M], ar[...])
        for h in range(2):
            sg[256 * h : 256 * h + 256, DS:W] = folded(last[64 * h : 64 * h + 64, :])
        order_y = (2, 1, 3, 0)
        for n, d in enumerate(order_y):
            group = rows((yh + d) % NYH, 32 * NX)
            sg[group, 0:DS] = t_dot(tg[0:MAIN, group], gi[:, 256:W]) + t_dot(tg[MAIN:M, group], ar[...])
            s_x[n] = sg[group, :].astype(BF)
            for k, (dx, dev) in enumerate(((2, x2), (1, xu), (3, xd))):
                push(s_x.at[n, rows((x + dx) % NX, 32), :], r_x.at[3 * n + k], x_s.at[0], x_r.at[n], dev)
        drain()
        sent(gcs, ex_s.at[1])
        sent(brs, ex_s.at[2])
        for n, d in enumerate(order_y):
            v = sg[rows(slot_c(d, 0), 32), :]
            arrived(r_x.at[pl.ds(3 * n, 3)], x_r.at[n])
            for k in range(3):
                v = v + r_x[3 * n + k].astype(F32)
            if d:
                s_y[n] = v.astype(BF)
                for c in range(2):
                    push(s_y.at[n, pl.ds(16 * c, 16), :], r_y.at[n], y_s.at[0], y_r.at[0], (at_img(d, 0) + c, cap))
            else:
                own_c[...] = v[0:16, :]
                o_s[...] = v[16:32, :]
                push(o_s, own_c, o_send.at[0], o_r.at[0], sib)
        sent(r_x, x_s.at[0])
        arrived(own_i, o_r.at[0])
        finish()
        sent(s_y, y_s.at[0])
        sent(o_s, o_send.at[0])

    @pl.when(core == 1)
    def _():
        arrived(gcs, ex_r.at[1])
        arrived(brs, ex_r.at[2])
        last = dot(tg[MAIN:M, 0:MAIN], gcs[...]) + dot(tg[MAIN:M, MAIN:M], brs[...])
        for h in range(2):
            sg[256 * h : 256 * h + 256, DS:W] = folded(last[64 * h : 64 * h + 64, :])
        for m in range(4):
            group = rows(2 * ((1 - yl) if m < 2 else yl) + m % 2, 128)
            sg[group, 0:DS] = dot(tg[group, 0:MAIN], gcs[...]) + dot(tg[group, MAIN:M], brs[...])
            if m == 1:
                for d in FAR_Z:
                    n = (z + d) % NZ
                    s_p[n] = sg[rows((1 - yl) * NZ + n, 32), :].astype(BF)
                    push(s_p.at[n], r_p.at[n], p_s.at[0], p_r.at[n], pair)
        drain()
        for d in FAR_Z:
            n = (z + d) % NZ
            arrived(r_p.at[n], p_r.at[n])
            v = sg[rows(yl * NZ + n, 32), :] + r_p[n].astype(F32)
            s_z[n] = v.astype(BF)

            @pl.when(z != n)
            def _():
                for c in range(2):
                    push(s_z.at[n, pl.ds(16 * c, 16), :], r_z.at[z], z_s.at[0], z_r.at[0], (chip + c, yl * NZ + n))

            @pl.when(z == n)
            def _():
                own_i[...] = v[16:32, :]
                o_s[...] = v[0:16, :]
                push(o_s, own_i, o_send.at[0], o_r.at[0], sib)

        sent(s_p, p_s.at[0])
        arrived(own_c, o_r.at[0])
        finish()
        sent(s_z.at[pl.ds(0, NZ - 1)], z_s.at[0])
        sent(o_s, o_send.at[0])


def local(image_student, caption_student, image_teacher, caption_teacher):
    vmem = pl.BlockSpec(memory_space=pltpu.VMEM)
    dma = pltpu.SemaphoreType.DMA
    out = pltpu.VMEM((B, DS), F32)
    args = [
        pltpu.with_memory_space_constraint(a, pltpu.HBM)
        for a in (image_student, caption_student, image_teacher, caption_teacher)
    ]
    return pl.pallas_call(
        kernel,
        out_shape=(out, out),
        in_specs=[pl.BlockSpec(memory_space=pltpu.HBM)] * 4,
        out_specs=(vmem, vmem),
        scratch_shapes=[
            pltpu.VMEM((B, DS), BF),
            pltpu.VMEM((B, DS), BF),
            pltpu.VMEM((B, DT), BF),
            pltpu.VMEM((B, DT), BF),
            pltpu.VMEM((4, 16, 256), F32),
            pltpu.VMEM((2, 2, 16, W), BF),
            pltpu.VMEM((MAIN, W), BF),
            pltpu.VMEM((MAIN, W), BF),
            pltpu.VMEM((M - MAIN, DS), BF),
            pltpu.VMEM((M - MAIN, DS), BF),
            pltpu.VMEM((MAIN, DS), BF),
            pltpu.VMEM((M - MAIN, DS), BF),
            pltpu.VMEM((2, M, M), F32),
            pltpu.VMEM((2, M, M), F32),
            pltpu.VMEM((2, M, M), F32),
            pltpu.VMEM((2, M, 1), F32),
            pltpu.VMEM((2, 1, M), F32),
            pltpu.VMEM((M, 128), F32),
            pltpu.VMEM((128, M), F32),
            pltpu.VMEM((2 * NR, 1, M), F32),
            pltpu.VMEM((2 * NQ, 1, M), F32),
            pltpu.VMEM((M, M), BF),
            pltpu.VMEM((MAIN, W), F32),
            pltpu.VMEM((NZ, 32, W), BF),
            pltpu.VMEM((NZ, 32, W), BF),
            pltpu.VMEM((NZ, 32, W), BF),
            pltpu.VMEM((NZ, 16, W), BF),
            pltpu.VMEM((NYH, 32 * NX, W), BF),
            pltpu.VMEM((3 * NYH, 32, W), BF),
            pltpu.VMEM((3, 32, W), BF),
            pltpu.VMEM((3, 16, W), BF),
            pltpu.VMEM((16, W), F32),
            pltpu.VMEM((16, W), F32),
            pltpu.VMEM((16, W), F32),
            dma((4,)), dma((2,)), dma((2,)), dma((NR,)), dma((NQ,)), dma((2,)), dma((2,)),
            dma((3,)), dma((3,)), dma((2,)), dma((1,)), dma((2,)), dma((1,)),
            dma((NZ,)), dma((1,)), dma((1,)), dma((1,)),
            dma((NYH,)), dma((1,)), dma((1,)), dma((1,)), dma((1,)), dma((1,)),
        ],
        compiler_params=pltpu.CompilerParams(
            collective_id=0, has_side_effects=True, vmem_limit_bytes=56 * 2**20
        ),
        cost_estimate=pl.CostEstimate(flops=1_800_000_000, bytes_accessed=400_000, transcendentals=1_700_000),
        name="contrastive",
    )(*args)


def solution(mesh):
    return jax.shard_map(
        local,
        mesh=mesh,
        in_specs=(
            P(("img", "cap"), None),
            P(("cap", "img"), None),
            P(("img", "cap"), None),
            P(("cap", "img"), None),
        ),
        out_specs=(P(("img", "cap"), None), P(("cap", "img"), None)),
        check_vma=False,
    )
```

```python
import math

import jax
import jax.numpy as jnp
from jax import lax
from jax.experimental import pallas as pl
from jax.experimental.pallas import tpu as pltpu
from jax.sharding import PartitionSpec as P

MESH = pl.DeviceIdType.MESH
GAIN = 3.0
NX, NYH, NZ = 4, 4, 8
NR = NQ = 16
DS, DT = 1024, 768
W = 256 + DS
WIDTH = (256 + DS, 256 + DT)
B = 20
MAIN, M = 32 * NR, 40 * NR
BF, F32 = jnp.bfloat16, jnp.float32
FAR_Z = (4, 3, 5, 2, 6, 1, 7, 0)
ORDER = "P0U1D1L0R0Y1Y3E1F1X0U2D2L1R1Y2E2L3R3F2U3D3X1R2L2E3F3X3U4X2F4"


def dot_t(a, b):
    return lax.dot_general(a, b, (((1,), (1,)), ((), ())), preferred_element_type=F32)


def t_dot(a, b):
    return lax.dot_general(a, b, (((0,), (0,)), ((), ())), preferred_element_type=F32)


def dot(a, b):
    return jnp.dot(a, b, preferred_element_type=F32)


def fold_matrix():
    a = lax.broadcasted_iota(jnp.int32, (256, 256), 0)
    b = lax.broadcasted_iota(jnp.int32, (256, 256), 1)
    source = 16 * ((a >> 2) & 15) + 4 * (a >> 6) + (a & 3)
    return jnp.where(b == source, 1.0, 0.0).astype(BF)


def pool(parts):
    m = jnp.max(parts, axis=0)
    return m + jnp.log(jnp.sum(jnp.exp(parts - m[None]), axis=0))


def kernel(
    is_hbm, cs_hbm, it_hbm, ct_hbm, oi_ref, oc_ref,
    is_ref, cs_ref, it_ref, ct_ref, rp, pk, gi, gc, ar, br, gcs, brs,
    sb, er, ec, rmx, cmx, tb, tb2, rxr, rxc, tg,
    sg, s_p, r_p, s_z, r_z, s_x, r_x, s_y, r_y, own_i, own_c, o_s,
    in_sem, sib_r, sib_s, gi_r, gc_r, first_s, next_s, ex_r, ex_s, lr_r, lr_s, lc_r, lc_s,
    p_r, p_s, z_r, z_s, x_r, x_s, y_r, y_s, o_r, o_send,
):
    img, cap = lax.axis_index("img"), lax.axis_index("cap")
    yh, x, core = img // (2 * NX), (img // 2) % NX, img % 2
    yl, z = cap // NZ, cap % NZ

    def at_img(dyh, dx):
        return (((yh + dyh) % NYH) * NX + (x + dx) % NX) * 2

    def slot_c(dyh, dx):
        return ((yh + dyh) % NYH) * NX + (x + dx) % NX

    def at_cap(dyl, dz):
        return ((yl + dyl) % 2) * NZ + (z + dz) % NZ

    def rows(slot, n):
        return pl.ds(pl.multiple_of(n * slot, n), n)

    def remote(src, dst, send, recv, dev):
        return pltpu.make_async_remote_copy(
            src_ref=src, dst_ref=dst, send_sem=send, recv_sem=recv, device_id=dev, device_id_type=MESH
        )

    def push(src, dst, send, recv, dev):
        remote(src, dst, send, recv, dev).start()

    def sent(ref, sem):
        remote(ref, ref, sem, in_sem.at[0], sib).wait_send()

    up, down, pair = (img, at_cap(0, 1)), (img, at_cap(0, -1)), (img, at_cap(1, 0))
    xu, xd, x2 = [(at_img(0, d) + core, cap) for d in (1, -1, 2)]
    ys = [(at_img(d, 0) + core, cap) for d in (1, 2, 3)]
    sib = (at_img(0, 0) + 1 - core, cap)

    def arrived(ref, sem):
        remote(ref, ref, in_sem.at[0], sem, sib).wait_recv()

    loads = []
    for n, (src, dst) in enumerate(((is_hbm, is_ref), (it_hbm, it_ref), (cs_hbm, cs_ref), (ct_hbm, ct_ref))):
        c = pltpu.make_async_copy(src, dst, in_sem.at[n])
        c.start()
        loads.append(c)

    barrier = pltpu.get_barrier_semaphore()
    chip = at_img(0, 0)
    around_i = [(chip, at_cap(1, 0)), (chip, at_cap(0, 1)), (chip, at_cap(0, -1))]
    around_c = [(at_img(*d), cap) for d in ((2, 0), (1, 0), (3, 0), (0, 1), (0, -1))]
    near = [sib] + [(dev[0] + c, dev[1]) for dev in around_i + around_c for c in range(2)]
    for dev in near:
        pl.semaphore_signal(barrier, inc=1, device_id=dev, device_id_type=MESH)

    def pack(j):
        for k, src, width in ((0, (is_ref, cs_ref)[j], DS), (1, (it_ref, ct_ref)[j], DT)):
            n = 2 * j + k
            loads[n].wait()
            pk[k, j, :, 256 : 256 + width] = src[0:16, :]
            if width < DS:
                pk[k, j, :, 256 + width : W] = jnp.zeros((16, DS - width), BF)
            last = src[...].astype(F32)[16:20, :]
            rp[n] = jnp.zeros((16, 256), F32)
            for q in range(width // 256):
                rp[n, 4 * q : 4 * q + 4, :] = last[:, 256 * q : 256 * q + 256]
            pk[k, j, :, 0:256] = rp[n].astype(BF)

    pack(0)

    @pl.when(core == 1)
    def _():
        gi[:, 256 + DT : W] = jnp.zeros((MAIN, DS - DT), BF)
        gc[:, 256 + DT : W] = jnp.zeros((MAIN, DS - DT), BF)

    pl.semaphore_wait(barrier, len(near))

    me_i, me_c = cap, slot_c(0, 0)
    mine_i, mine_c = rows(2 * me_i + core, 16), rows(2 * me_c + core, 16)
    for dev in around_i:
        for k, width in enumerate(WIDTH):
            w = pl.ds(0, width)
            push(pk.at[k, 0, :, w], gi.at[mine_i, w], first_s.at[k], gi_r.at[me_i], (dev[0] + k, dev[1]))

    pack(1)

    def own_caption(dev):
        for k, width in enumerate(WIDTH):
            w = pl.ds(0, width)
            push(pk.at[k, 1, :, w], gc.at[mine_c, w], first_s.at[k], gc_r.at[me_c], (dev[0] + k, dev[1]))

    for dev in around_c[3:] + around_c[1:3]:
        own_caption(dev)
    for k, width in enumerate(WIDTH):

        @pl.when(core != k)
        def _():
            w = pl.ds(0, width)
            push(pk.at[k, 0, :, w], gi.at[mine_i, w], sib_s.at[0], sib_r.at[0], sib)
            push(pk.at[k, 1, :, w], gc.at[mine_c, w], sib_s.at[1], sib_r.at[1], sib)

    gi[mine_i, :] = pk[core, 0]
    gc[mine_c, :] = pk[core, 1]

    flow = {}
    for k in (1, 2, 3):
        flow["U%d" % k] = (at_cap(0, -k), (up,))
        flow["D%d" % k] = (at_cap(0, k), (down,) if k < 3 else ())
        flow["E%d" % k] = (at_cap(1, -k), (up,) if k < 3 else ())
        flow["F%d" % k] = (at_cap(1, k), (down,))
    flow["P0"] = (at_cap(1, 0), (up, down))
    flow["U4"] = (at_cap(0, -4), ())
    flow["F4"] = (at_cap(1, 4), ())
    for j in range(NYH):
        if j:
            flow["Y%d" % j] = (slot_c(j, 0), (xu, xd))
        flow["L%d" % j] = (slot_c(j, -1), (xu,) if j < 2 else ())
        flow["R%d" % j] = (slot_c(j, 1), (xd,) if j >= 2 else ())
        flow["X%d" % j] = (slot_c(j, 2), ())

    def caption(slot):
        push(gc.at[rows(slot, 32), pl.ds(256, DS)], gcs.at[rows(slot, 32), :], ex_s.at[1], ex_r.at[1], sib)

    for k, width in enumerate(WIDTH):

        @pl.when(core == k)
        def _():
            for n in range(0, len(ORDER), 2):
                name = ORDER[n : n + 2]
                if n == 6:
                    own_caption(around_c[0])
                    arrived(gi.at[rows(2 * me_i + 1 - core, 16), pl.ds(0, width)], sib_r.at[0])
                    arrived(gc.at[rows(2 * me_c + 1 - core, 16), pl.ds(0, width)], sib_r.at[1])
                slot, devs = flow[name]
                buf, recv, send = (gc, gc_r, next_s.at[1]) if name[0] in "YLRX" else (gi, gi_r, next_s.at[0])
                block = buf.at[rows(slot, 32), pl.ds(0, width)]
                arrived(block, recv.at[slot])
                for dev in devs:
                    push(block, block, send, recv.at[slot], dev)
                if k == 0 and n == len(ORDER) - 12:
                    for j in range(NYH):
                        for d in (0, 1, 3) if j > 1 else range(NX):
                            caption(slot_c(j, d))
                if k == 0 and name[0] == "X" and n > len(ORDER) - 12:
                    caption(slot)

    fold = fold_matrix()
    for src, dst in ((gi, ar), (gc, br)):
        for h in range(2):
            y = dot(fold, src[256 * h : 256 * h + 256, 0:256]).astype(BF)
            for q in range(4):
                dst[64 * h : 64 * h + 64, 256 * q : 256 * q + 256] = y[64 * q : 64 * q + 64, :]

    @pl.when(core == 0)
    def _():
        push(br, brs, ex_s.at[2], ex_r.at[2], sib)

    gain = jnp.where(core == 0, GAIN / math.sqrt(DS), GAIN / math.sqrt(DT))
    sb[core, 0:MAIN, 0:MAIN] = gain * dot_t(gi[:, 256:W], gc[:, 256:W])
    sb[core, 0:MAIN, MAIN:M] = gain * dot_t(gi[:, 256:W], br[...])
    sb[core, MAIN:M, 0:MAIN] = gain * dot_t(ar[...], gc[:, 256:W])
    sb[core, MAIN:M, MAIN:M] = gain * dot_t(ar[...], br[...])
    push(sb.at[core], sb.at[core], ex_s.at[0], ex_r.at[0], sib)

    def statistics(k):
        top, total, lses = None, None, []
        for b in range(0, M, 64):
            blk = sb[k, b : b + 64, :]
            m = jnp.max(blk, axis=1, keepdims=True)
            rmx[k, b : b + 64, :] = m
            e = jnp.exp(blk - m)
            er[k, b : b + 64, :] = e
            lses.append(m + jnp.log(jnp.sum(e, axis=1, keepdims=True)))
            t = jnp.max(blk, axis=0, keepdims=True)
            top = t if top is None else jnp.maximum(top, t)
        for b in range(0, M, 64):
            e = jnp.exp(sb[k, b : b + 64, :] - top)
            ec[k, b : b + 64, :] = e
            t = jnp.sum(e, axis=0, keepdims=True)
            total = t if total is None else total + t
        cmx[k] = top
        return lses, top + jnp.log(total)

    row_lse, col_lse = statistics(core)

    rxc[core * NQ + me_c] = col_lse
    for n, b in enumerate(range(0, M, 64)):
        tb[b : b + 64, :] = jnp.broadcast_to(row_lse[n], (64, 128))
    rxr[core * NR + me_i] = tb[...].T[0:1, :]
    mine_c, mine_r = rxc.at[core * NQ + me_c], rxr.at[core * NR + me_i]
    far = [(2 * min(j, 4 - j) + min(d, 4 - d), j, d, True) for j in range(NYH) for d in range(NX)]
    far += [(j + min(d, 8 - d), j, d, False) for j in range(2) for d in range(NZ)]
    for hops, j, d, of_columns in sorted(far, reverse=True):
        if hops:
            for c in range(2):
                if of_columns:
                    push(mine_c, mine_c, lc_s.at[0], lc_r.at[core], (at_img(j, d) + c, cap))
                else:
                    push(mine_r, mine_r, lr_s.at[0], lr_r.at[core], (chip + c, at_cap(j, d)))
    push(mine_c, mine_c, lc_s.at[0], lc_r.at[core], sib)
    push(mine_r, mine_r, lr_s.at[0], lr_r.at[core], sib)

    tb2[...] = jnp.zeros_like(tb2)
    for k, width in enumerate(WIDTH):
        sent(gi.at[pl.ds(0, 128), pl.ds(0, width)], first_s.at[k])

        @pl.when(core == k)
        def _():
            sent(gi.at[pl.ds(0, 384), pl.ds(0, width)], next_s.at[0])
            sent(gc.at[pl.ds(0, 320), pl.ds(0, width)], next_s.at[1])

        @pl.when(core != k)
        def _():
            for n in range(2):
                sent(gi.at[pl.ds(0, 16), pl.ds(0, width)], sib_s.at[n])

    arrived(sb.at[1 - core], ex_r.at[0])
    statistics(1 - core)

    arrived(rxc.at[pl.ds(0, NQ - 1)], lc_r.at[core])
    arrived(rxc.at[pl.ds(0, NQ)], lc_r.at[1 - core])
    arrived(rxr.at[pl.ds(0, NR - 1)], lr_r.at[core])
    arrived(rxr.at[pl.ds(0, NR)], lr_r.at[1 - core])
    tb2[0:1, :] = pool(rxr[0:NR])
    tb2[1:2, :] = pool(rxr[NR : 2 * NR])
    rows_all = tb2[...].T
    f_col_s = 0.5 * jnp.exp(cmx[0] - pool(rxc[0:NQ]))
    f_col_t = 0.25 * jnp.exp(cmx[1] - pool(rxc[NQ : 2 * NQ]))

    b = lax.broadcasted_iota(jnp.int32, (1, M), 1)
    t = jnp.where(b < MAIN, b >> 4, (b - MAIN) >> 2)
    u = jnp.where(b < MAIN, b & 15, 16 + (b & 3))
    col_id = cap * M + t * B + u
    for lo in range(0, M, 64):
        a = lo + lax.broadcasted_iota(jnp.int32, (64, 1), 0)
        t, u = (a >> 4, a & 15) if lo < MAIN else ((a - MAIN) >> 2, 16 + (a & 3))
        row_id = (at_img(0, 0) + (t & 1)) * (B * NR) + (t >> 1) * B + u
        here = slice(lo, lo + 64)
        f_row_s = 0.5 * jnp.exp(rmx[0, here, :] - rows_all[here, 0:1])
        f_row_t = 0.25 * jnp.exp(rmx[1, here, :] - rows_all[here, 1:2])
        g = er[0, here, :] * f_row_s + ec[0, here, :] * f_col_s
        g = g - (er[1, here, :] * f_row_t + ec[1, here, :] * f_col_t)
        g = g - jnp.where(row_id == col_id, 0.5, 0.0)
        tg[here, :] = g.astype(BF)

    def folded(v):
        v = jnp.concatenate([v[:, 256 * q : 256 * q + 256] for q in range(4)], axis=0)
        hi = v.astype(BF)
        lo = (v - hi.astype(F32)).astype(BF)
        return t_dot(fold, hi) + t_dot(fold, lo)

    def unfold(acc, out):
        out[0:16, :] = acc[:, 0:DS]
        for q in range(4):
            out[16:20, 256 * q : 256 * q + 256] = acc[4 * q : 4 * q + 4, DS:W]

    def finish():
        arrived(r_y, y_r.at[0])
        acc = own_c[...]
        for n in range(3):
            acc = acc + r_y[n].astype(F32)
        unfold(acc, oc_ref)
        arrived(r_z.at[pl.ds(0, NZ - 1)], z_r.at[0])
        r_z[z] = jnp.zeros((16, W), BF)
        acc = own_i[...]
        for n in range(NZ):
            acc = acc + r_z[n].astype(F32)
        unfold(acc, oi_ref)

    def drain():
        sent(sb.at[0], ex_s.at[0])
        sent(rxr.at[pl.ds(0, 2 * NR - 1)], lr_s.at[0])
        sent(rxc.at[pl.ds(0, 2 * NQ - 1)], lc_s.at[0])

    @pl.when(core == 0)
    def _():
        last = t_dot(tg[0:MAIN, MAIN:M], gi[:, 256:W]) + t_dot(tg[MAIN:M, MAIN:M], ar[...])
        for h in range(2):
            sg[256 * h : 256 * h + 256, DS:W] = folded(last[64 * h : 64 * h + 64, :])
        order_y = (2, 1, 3, 0)
        for n, d in enumerate(order_y):
            group = rows((yh + d) % NYH, 32 * NX)
            sg[group, 0:DS] = t_dot(tg[0:MAIN, group], gi[:, 256:W]) + t_dot(tg[MAIN:M, group], ar[...])
            s_x[n] = sg[group, :].astype(BF)
            for k, (dx, dev) in enumerate(((2, x2), (1, xu), (3, xd))):
                push(s_x.at[n, rows((x + dx) % NX, 32), :], r_x.at[3 * n + k], x_s.at[0], x_r.at[n], dev)
        drain()
        sent(gcs, ex_s.at[1])
        sent(brs, ex_s.at[2])
        for n, d in enumerate(order_y):
            v = sg[rows(slot_c(d, 0), 32), :]
            arrived(r_x.at[pl.ds(3 * n, 3)], x_r.at[n])
            for k in range(3):
                v = v + r_x[3 * n + k].astype(F32)
            if d:
                s_y[n] = v.astype(BF)
                for c in range(2):
                    push(s_y.at[n, pl.ds(16 * c, 16), :], r_y.at[n], y_s.at[0], y_r.at[0], (at_img(d, 0) + c, cap))
            else:
                own_c[...] = v[0:16, :]
                o_s[...] = v[16:32, :]
                push(o_s, own_c, o_send.at[0], o_r.at[0], sib)
        sent(r_x, x_s.at[0])
        arrived(own_i, o_r.at[0])
        finish()
        sent(s_y, y_s.at[0])
        sent(o_s, o_send.at[0])

    @pl.when(core == 1)
    def _():
        arrived(gcs, ex_r.at[1])
        arrived(brs, ex_r.at[2])
        last = dot(tg[MAIN:M, 0:MAIN], gcs[...]) + dot(tg[MAIN:M, MAIN:M], brs[...])
        for h in range(2):
            sg[256 * h : 256 * h + 256, DS:W] = folded(last[64 * h : 64 * h + 64, :])
        for m in range(4):
            group = rows(2 * ((1 - yl) if m < 2 else yl) + m % 2, 128)
            sg[group, 0:DS] = dot(tg[group, 0:MAIN], gcs[...]) + dot(tg[group, MAIN:M], brs[...])
            if m == 1:
                for d in FAR_Z:
                    n = (z + d) % NZ
                    s_p[n] = sg[rows((1 - yl) * NZ + n, 32), :].astype(BF)
                    push(s_p.at[n], r_p.at[n], p_s.at[0], p_r.at[n], pair)
        drain()
        for d in FAR_Z:
            n = (z + d) % NZ
            arrived(r_p.at[n], p_r.at[n])
            v = sg[rows(yl * NZ + n, 32), :] + r_p[n].astype(F32)
            s_z[n] = v.astype(BF)

            @pl.when(z != n)
            def _():
                for c in range(2):
                    push(s_z.at[n, pl.ds(16 * c, 16), :], r_z.at[z], z_s.at[0], z_r.at[0], (chip + c, yl * NZ + n))

            @pl.when(z == n)
            def _():
                own_i[...] = v[16:32, :]
                o_s[...] = v[0:16, :]
                push(o_s, own_i, o_send.at[0], o_r.at[0], sib)

        sent(s_p, p_s.at[0])
        arrived(own_c, o_r.at[0])
        finish()
        sent(s_z.at[pl.ds(0, NZ - 1)], z_s.at[0])
        sent(o_s, o_send.at[0])


def local(image_student, caption_student, image_teacher, caption_teacher):
    vmem = pl.BlockSpec(memory_space=pltpu.VMEM)
    dma = pltpu.SemaphoreType.DMA
    out = pltpu.VMEM((B, DS), F32)
    args = [
        pltpu.with_memory_space_constraint(a, pltpu.HBM)
        for a in (image_student, caption_student, image_teacher, caption_teacher)
    ]
    return pl.pallas_call(
        kernel,
        out_shape=(out, out),
        in_specs=[pl.BlockSpec(memory_space=pltpu.HBM)] * 4,
        out_specs=(vmem, vmem),
        scratch_shapes=[
            pltpu.VMEM((B, DS), BF),
            pltpu.VMEM((B, DS), BF),
            pltpu.VMEM((B, DT), BF),
            pltpu.VMEM((B, DT), BF),
            pltpu.VMEM((4, 16, 256), F32),
            pltpu.VMEM((2, 2, 16, W), BF),
            pltpu.VMEM((MAIN, W), BF),
            pltpu.VMEM((MAIN, W), BF),
            pltpu.VMEM((M - MAIN, DS), BF),
            pltpu.VMEM((M - MAIN, DS), BF),
            pltpu.VMEM((MAIN, DS), BF),
            pltpu.VMEM((M - MAIN, DS), BF),
            pltpu.VMEM((2, M, M), F32),
            pltpu.VMEM((2, M, M), F32),
            pltpu.VMEM((2, M, M), F32),
            pltpu.VMEM((2, M, 1), F32),
            pltpu.VMEM((2, 1, M), F32),
            pltpu.VMEM((M, 128), F32),
            pltpu.VMEM((128, M), F32),
            pltpu.VMEM((2 * NR, 1, M), F32),
            pltpu.VMEM((2 * NQ, 1, M), F32),
            pltpu.VMEM((M, M), BF),
            pltpu.VMEM((MAIN, W), F32),
            pltpu.VMEM((NZ, 32, W), BF),
            pltpu.VMEM((NZ, 32, W), BF),
            pltpu.VMEM((NZ, 32, W), BF),
            pltpu.VMEM((NZ, 16, W), BF),
            pltpu.VMEM((NYH, 32 * NX, W), BF),
            pltpu.VMEM((3 * NYH, 32, W), BF),
            pltpu.VMEM((3, 32, W), BF),
            pltpu.VMEM((3, 16, W), BF),
            pltpu.VMEM((16, W), F32),
            pltpu.VMEM((16, W), F32),
            pltpu.VMEM((16, W), F32),
            dma((4,)), dma((2,)), dma((2,)), dma((NR,)), dma((NQ,)), dma((2,)), dma((2,)),
            dma((3,)), dma((3,)), dma((2,)), dma((1,)), dma((2,)), dma((1,)),
            dma((NZ,)), dma((1,)), dma((1,)), dma((1,)),
            dma((NYH,)), dma((1,)), dma((1,)), dma((1,)), dma((1,)), dma((1,)),
        ],
        compiler_params=pltpu.CompilerParams(
            collective_id=0, has_side_effects=True, vmem_limit_bytes=56 * 2**20
        ),
        cost_estimate=pl.CostEstimate(flops=1_800_000_000, bytes_accessed=400_000, transcendentals=1_700_000),
        name="contrastive",
    )(*args)


def solution(mesh):
    return jax.shard_map(
        local,
        mesh=mesh,
        in_specs=(
            P(("img", "cap"), None),
            P(("cap", "img"), None),
            P(("img", "cap"), None),
            P(("cap", "img"), None),
        ),
        out_specs=(P(("img", "cap"), None), P(("cap", "img"), None)),
        check_vma=False,
    )
```
